1024 devices in a mesh: wave: 64 (over z_hi, x, core), lev: 16 (over y, z_lo).
Axes of the slice: x: 8, y: 8, z: 8 (z_hi: 4, z_lo: 2; z = z_hi * 2 + z_lo), core: 2. Of those that a mesh axis runs over, the one named last changes fastest.
Arguments:
- spectral: bfloat16 [320, 2, 64, 641], P('wave', None, 'lev'), may hold values from -6 to 6
- legendre: bfloat16 [320, 641, 640], P('wave'), as said below
- quad_weights: float32 [640], replicated, as said below
- pair_order: int32 [320], replicated, may hold values from 0 to 319, as said below
- lon_counts: int32 [1280], replicated, may hold values from 20 to 2560
- vertical: bfloat16 [64, 64], replicated, may hold values from -0.75 to 0.75
- wind_field: bfloat16 [1280, 64, 2560], P('wave', 'lev'), may hold values from -6 to 6
Outputs:
- spectral_tendency: float32 [320, 2, 64, 641], P('wave', None, 'lev')
The draws below stay inside these ranges and needn't reach their ends.
Inputs may be any that keep to these rules, and one draw needn't show every extreme that they name: Each pair index appears once; slot s holds the wavenumbers pair_order[s] and 639 - pair_order[s], and the rows of spectral and legendre in slot s follow it. legendre[s, r, j] is the associated Legendre function of row r's degree and wavenumber, normalized so that the integral of its square over mu = cos(colatitude) from -1 to 1 is 1, at the node j of quad_weights; the southern node 1279 - j mirrors node j. `quad_weights`: Positive.
All inputs are finite; a program needn't handle non-finite values.
Results may differ from the reference program's by a relative error of at most 0.0077.
Values may be sent and summed in bfloat16 or wider, within the bound.
A program may use at most 32 MiB of HBM per device.

```python
import math
import jax
import jax.numpy as jnp
from jax import lax

M = 640
NLAT = 1280
NLON = 2560
LEVELS = 64
PAIRS = 320
ROWS = 641
NHALF = 640
N_WAVE = 64


def latitude_nodes(key):
    jitter_key = jax.random.fold_in(key, 11)
    weight_key = jax.random.fold_in(key, 12)
    jitter = jax.random.uniform(jitter_key, (NHALF,), jnp.float32, -0.25, 0.25)
    spread = jax.random.uniform(weight_key, (NHALF,), jnp.float32, 0.7, 1.3)
    colatitude = math.pi * (jnp.arange(NHALF, dtype=jnp.float32) + 0.5 + jitter) / NLAT
    sine_values = jnp.sin(colatitude)
    return (jnp.cos(colatitude), sine_values, math.pi / NLAT * sine_values * spread)


def pair_permutation(key):
    return jax.random.permutation(jax.random.fold_in(key, 21), PAIRS).astype(jnp.int32)


def draw_pair_order(key, part):
    return pair_permutation(key)


def draw_quad_weights(key, part):
    return latitude_nodes(key)[2].astype(jnp.float32)


def draw_lon_counts(key, part):
    lat_index = jnp.arange(NLAT, dtype=jnp.int32)
    distance = jnp.minimum(lat_index, NLAT - 1 - lat_index)
    jitter_steps = jax.random.randint(jax.random.fold_in(key, 31), (NLAT,), 0, 4)
    return jnp.minimum(NLON, 20 + 4 * distance + 4 * jitter_steps).astype(jnp.int32)


def draw_legendre(key, part):
    cosines, sine_values, _ = latitude_nodes(key)
    permuted = pair_permutation(key)
    orders = jnp.arange(1, M, dtype=jnp.float32)
    log_steps = 0.5 * jnp.log((2.0 * orders + 1.0) / (2.0 * orders))
    diag_log = jnp.concatenate([jnp.zeros((1,), jnp.float32), jnp.cumsum(log_steps)]) + 0.5 * math.log(0.5)
    log_sines = jnp.log(sine_values)

    def one_pair(low_wave):
        pair_waves = jnp.stack([low_wave, M - 1 - low_wave])
        degrees = pair_waves.astype(jnp.float32)
        diagonal_start = jnp.exp(diag_log[pair_waves][:, None] + degrees[:, None] * log_sines[None, :])

        def advance(recurrence, degree):
            prev_one, prev_two = recurrence
            degree_value = degree.astype(jnp.float32)
            alpha_coef = jnp.sqrt((4.0 * degree_value ** 2 - 1.0) / jnp.maximum(degree_value ** 2 - degrees ** 2, 1.0))
            beta_coef = jnp.sqrt(jnp.maximum((degree_value - 1.0) ** 2 - degrees ** 2, 0.0) / jnp.maximum(4.0 * (degree_value - 1.0) ** 2 - 1.0, 1.0))
            recurred = alpha_coef[:, None] * (cosines[None, :] * prev_one - beta_coef[:, None] * prev_two)
            above = (degree_value > degrees)[:, None]
            equal = (degree_value == degrees)[:, None]
            current = jnp.where(equal, diagonal_start, jnp.where(above, recurred, 0.0))
            return ((current, prev_one), current)
        zeros_start = jnp.zeros((2, NHALF), jnp.float32)
        _, values = lax.scan(advance, (zeros_start, zeros_start), jnp.arange(M, dtype=jnp.int32))
        row_ids = jnp.arange(M + 1, dtype=jnp.int32)
        in_first = row_ids < M - low_wave
        degree_index = jnp.where(in_first, low_wave + row_ids, row_ids - 1)
        which_wave = jnp.where(in_first, 0, 1)
        return values[degree_index, which_wave]
    packed = lax.map(one_pair, permuted)
    return packed.astype(jnp.bfloat16)


def levels(stream_key, extent, split, low, largest):
    factor_of = 1.0
    for position, shards_of in split:
        heights = jax.random.uniform(jax.random.fold_in(jax.random.fold_in(stream_key, 6), position), (shards_of,), jnp.float32, low / len(split), largest / len(split))
        factor_of = factor_of * jnp.repeat(jnp.exp(heights), extent[position] // shards_of).reshape((-1,) + (1,) * (len(extent) - 1 - position))
    return factor_of


def noise(key, extent, scale, bound, split=(), kind=jnp.bfloat16):
    level = levels(key, extent, split, -0.22, 0.18) if split else 1.0
    result = jax.random.normal(key, extent, jnp.float32) * scale * level
    return jnp.minimum(jnp.maximum(result, -bound), bound).astype(kind)


def setup_inputs(seed: int = 0) -> dict:
    streams_of = jax.random.split(jax.random.key(seed), 8)
    spectral = noise(streams_of[0], (PAIRS, 2, LEVELS, ROWS), 1.0, 6.0, ((0, 64), (2, 16)))
    legendre = draw_legendre(jax.random.fold_in(streams_of[7], 71), 0)
    quad_weights = draw_quad_weights(jax.random.fold_in(streams_of[7], 71), 0)
    pair_order = draw_pair_order(jax.random.fold_in(streams_of[7], 71), 0)
    lon_counts = draw_lon_counts(jax.random.fold_in(streams_of[7], 71), 0)
    vertical = noise(streams_of[5], (LEVELS, LEVELS), LEVELS ** -0.5, 0.75)
    wind_field = noise(streams_of[6], (NLAT, LEVELS, NLON), 1.0, 6.0, ((0, 64), (1, 16)))
    return {"spectral": spectral, "legendre": legendre, "quad_weights": quad_weights, "pair_order": pair_order, "lon_counts": lon_counts, "vertical": vertical, "wind_field": wind_field}


def row_layout(low_waves, row_count, total_waves):
    row_ids = jnp.arange(row_count, dtype=jnp.int32)[None, :]
    in_first = row_ids < (total_waves - low_waves[:, None])
    degree_gap = jnp.where(in_first, row_ids, row_ids - total_waves + low_waves[:, None])
    return in_first.astype(jnp.float32), (degree_gap % 2).astype(jnp.float32)


def fourier_basis(wavenumbers, lon_count):
    longitudes = jnp.arange(lon_count, dtype=jnp.int32)
    phases = (wavenumbers[:, None] * longitudes[None, :]) % lon_count
    angles = phases.astype(jnp.float32) * (2.0 * math.pi / lon_count)
    factor = jnp.where(wavenumbers == 0, 1.0, 2.0).astype(jnp.float32)
    basis = jnp.stack([factor[:, None] * jnp.cos(angles), -factor[:, None] * jnp.sin(angles)], axis=1)
    return basis.astype(jnp.bfloat16), factor


def reference(spectral, legendre, quad_weights, pair_order, lon_counts, vertical, wind_field):
    first_part, parity = row_layout(pair_order, M + 1, M)
    slot_pick = jnp.stack([first_part, 1.0 - first_part], axis=1)
    parity_pick = jnp.stack([1.0 - parity, parity], axis=1)
    vertical_wide = vertical.astype(jnp.float32)
    mixed = jnp.einsum("kl,pclr->pckr", vertical_wide, spectral.astype(jnp.float32)).astype(jnp.bfloat16)

    def inverse_pair(inputs):
        coefs, table_rows, slots, parities = inputs
        selector = slots[:, None, :] * parities[None, :, :]
        masked = selector[:, :, None, None, :] * coefs.astype(jnp.float32)[None, None]
        partial_value = jnp.einsum("tqrlx,xj->tqrlj", masked, table_rows.astype(jnp.float32))
        symmetric = partial_value[:, 0]
        antisymmetric = partial_value[:, 1]
        joined = jnp.concatenate([symmetric + antisymmetric, (symmetric - antisymmetric)[..., ::-1]], axis=-1)
        return joined.astype(jnp.bfloat16)

    fourier = lax.map(inverse_pair, (mixed, legendre, slot_pick, parity_pick)).reshape(M, 2, LEVELS, NLAT)
    wavenumbers = jnp.stack([pair_order, M - 1 - pair_order], axis=1).reshape(M)
    basis, factor = fourier_basis(wavenumbers, NLON)
    basis_wide = basis.astype(jnp.float32)
    band_lats = NLAT // N_WAVE
    blocks = jnp.moveaxis(fourier.reshape(M, 2, LEVELS, N_WAVE, band_lats), 3, 0)
    wind_blocks = wind_field.reshape(N_WAVE, band_lats, LEVELS, NLON)
    count_blocks = lon_counts.reshape(N_WAVE, band_lats)

    def grid_band(inputs):
        coefs, winds, counts = inputs
        retained = (2 * wavenumbers[:, None] < counts[None, :]).astype(jnp.float32)
        masked = coefs.astype(jnp.float32) * retained[:, None, None, :]
        grid_values = jnp.einsum("mrlj,mrn->jln", masked, basis_wide).astype(jnp.bfloat16)
        grid_values = lax.optimization_barrier(grid_values)
        forcing = (winds.astype(jnp.float32) * grid_values.astype(jnp.float32)).astype(jnp.bfloat16)
        transformed = jnp.einsum("jln,mrn->mrlj", forcing.astype(jnp.float32), basis_wide)
        rescale = retained / (factor[:, None] * NLON)
        return (transformed * rescale[:, None, None, :]).astype(jnp.bfloat16)

    returned = lax.map(grid_band, (blocks, wind_blocks, count_blocks))
    fourier_back = jnp.moveaxis(returned, 0, 3).reshape(PAIRS, 2, 2, LEVELS, NLAT)

    def forward_pair(inputs):
        coefs, table_rows, slots, parities = inputs
        northern = coefs[..., :NHALF].astype(jnp.float32)
        southern = coefs[..., NHALF:][..., ::-1].astype(jnp.float32)
        even_part = ((northern + southern) * quad_weights).astype(jnp.bfloat16)
        odd_part = ((northern - southern) * quad_weights).astype(jnp.bfloat16)
        folded = jnp.stack([even_part, odd_part], axis=1).astype(jnp.float32)
        products = jnp.einsum("xj,tqrlj->tqrlx", table_rows.astype(jnp.float32), folded)
        selector = slots[:, None, :] * parities[None, :, :]
        return jnp.sum(products * selector[:, :, None, None, :], axis=(0, 1))

    return lax.map(forward_pair, (fourier_back, legendre, slot_pick, parity_pick))
```

```python
import math

import jax
import jax.numpy as jnp
from jax import lax
from jax.experimental import pallas as pl
from jax.experimental.pallas import tpu as pltpu
from jax.sharding import PartitionSpec as P

MESH = pl.DeviceIdType.MESH
F32 = jnp.float32
BF16 = jnp.bfloat16

WAVES = 64
LEVS = 16
SLOTS = 5
LEVELS = 4
TOTAL = 640
BAND = 20
LONS = 2560
HALF = LONS // 2
TILE = 16
COLS = 2 * SLOTS * 2 * WAVES


def dot(a, b):
    return jnp.dot(a, b, preferred_element_type=F32)


def dot_nt(a, b):
    return lax.dot_general(a, b, (((1,), (1,)), ((), ())), preferred_element_type=F32)


def iota(shape, dim):
    return lax.broadcasted_iota(jnp.int32, shape, dim)


def rows_at(start, size=TILE):
    return pl.ds(pl.multiple_of(start, TILE), size)


def half_angle(phase):
    wrapped = phase - float(LONS) * jnp.floor(phase * (1.0 / LONS) + 0.5)
    u = wrapped * (math.pi / LONS)
    q = u * u
    sine = u * (
        1.0
        + q * (-1 / 6 + q * (1 / 120 + q * (-1 / 5040 + q * (1 / 362880 + q * (-1 / 39916800)))))
    )
    cosine = 1.0 + q * (
        -1 / 2
        + q * (1 / 24 + q * (-1 / 720 + q * (1 / 40320 + q * (-1 / 3628800 + q * (1 / 479001600)))))
    )
    return 1.0 - 2.0 * sine * sine, 2.0 * sine * cosine


def group_row(row, half):
    g, rho = (row - 80 * half) // TILE, row % TILE
    last = g == 4
    s = jnp.where(last, 4, (rho // 2) % 4)
    t = rho % 2
    c = jnp.where(last, (rho // 2) % 2, rho // 8)
    level = jnp.where(last, rho // 4, g)
    return 32 * s + 16 * t + 8 * half + 4 * c + level


def kernel(
    spec_ref,
    leg_hbm,
    qw_ref,
    pair_ref,
    cnt_ref,
    vert_ref,
    wind_hbm,
    out_ref,
    leg_v,
    wind_v,
    wind_f,
    mixm,
    s1f,
    s1,
    r1,
    s2,
    r2,
    basis,
    keep_even,
    keep_odd,
    back_even,
    back_odd,
    fb,
    hs,
    sel_out,
    sel_in,
    s3,
    r3,
    xt,
    ff,
    fp,
    bk,
    s5,
    r5,
    dup,
    local_sem,
    send_sem,
    recv_sem,
):
    w = lax.axis_index("wave")
    v = lax.axis_index("lev")
    north = w < WAVES // 2

    barrier = pltpu.get_barrier_semaphore()

    @pl.loop(1, LEVS)
    def _(i):
        pl.semaphore_signal(barrier, 1, device_id={"lev": lax.rem(v + i, LEVS)}, device_id_type=MESH)

    @pl.loop(1, WAVES)
    def _(i):
        pl.semaphore_signal(barrier, 1, device_id={"wave": lax.rem(w + i, WAVES)}, device_id_type=MESH)

    leg_copy = pltpu.make_async_copy(leg_hbm, leg_v, local_sem.at[0])
    leg_copy.start()
    wind_copy = pltpu.make_async_copy(wind_hbm, wind_v, local_sem.at[1])
    wind_copy.start()

    first_lane = iota((LEVELS, 128), 1) == 0

    @pl.loop(0, SLOTS)
    def _(s):
        for chunk in range(6):
            for c in range(2):
                if chunk < 5:
                    piece = spec_ref[s, c, :, 128 * chunk : 128 * chunk + 128].astype(F32)
                else:
                    column = spec_ref[s, c, :, TOTAL : TOTAL + 1].astype(F32)
                    piece = jnp.where(first_lane, jnp.broadcast_to(column, (LEVELS, 128)), 0.0)
                at = 8 * (chunk % 2) + 4 * c
                s1f[3 * s + chunk // 2, at : at + LEVELS, :] = piece

    s1f[15] = jnp.zeros((TILE, 128), F32)
    s1[...] = s1f[...].reshape(256, 128).astype(BF16)

    pick = (iota((256, 64), 1) == 4 * (iota((256, 64), 0) // 16) + iota((256, 64), 0) % 4).astype(BF16)
    spread = dot_nt(dot(pick, vert_ref[...]).astype(BF16), pick)
    same = (iota((256, 256), 0) // 4) % 4 == (iota((256, 256), 1) // 4) % 4
    mixm[...] = jnp.where(same, spread, 0.0).astype(BF16)

    pl.semaphore_wait(barrier, LEVS - 1 + WAVES - 1)

    def lev_send(phase, source, target):
        @pl.loop(1, LEVS)
        def _(i):
            d = lax.rem(v + i, LEVS)
            pltpu.make_async_remote_copy(
                src_ref=source.at[rows_at(TILE * d)],
                dst_ref=target.at[rows_at(TILE * v)],
                send_sem=send_sem.at[phase],
                recv_sem=recv_sem.at[phase],
                device_id={"lev": d},
                device_id_type=MESH,
            ).start()

        pltpu.make_async_copy(
            source.at[rows_at(TILE * v)], target.at[rows_at(TILE * v)], recv_sem.at[phase]
        ).start()

    def all_landed(phase, target):
        pltpu.make_async_copy(target, target, recv_sem.at[phase]).wait()

    def all_sent(phase, source):
        part = source.at[pl.ds(0, source.shape[0] - TILE)]
        pltpu.make_async_copy(part, part, send_sem.at[phase]).wait()

    lane8 = iota((8, 128), 1)
    row8 = iota((8, 128), 0)
    group8 = lane8 // BAND
    lat_of = lane8 % BAND
    counts = jnp.zeros((8, 128), jnp.int32)
    for jj in range(BAND):
        lat = jnp.where(north, BAND * w + jj, BAND * w + BAND - 1 - jj)
        counts = jnp.where(lat_of == jj, cnt_ref[lat], counts)
    counts = jnp.where(group8 < 5, counts, 0)

    def wave_rows(first, stride):
        m = jnp.zeros((8, 128), jnp.int32)
        for i in range(4):
            m = jnp.where(row8 // 2 == i, pair_ref[first + stride * i], m)
        return jnp.where(row8 % 2 == 1, TOTAL - 1 - m, m)

    def make_rows(tile, m):
        mf = m.astype(F32)
        factor = jnp.where(m == 0, 1.0, 2.0)
        cos0, sin0 = half_angle(mf * lane8.astype(F32))
        turn_c, turn_s = half_angle(mf * 128.0)
        real, imag = factor * cos0, -factor * sin0
        for a in range(HALF // 128):
            basis[rows_at(TILE * tile), 128 * a : 128 * a + 128] = jnp.concatenate(
                [real, imag], axis=0
            ).astype(BF16)
            if a + 1 < HALF // 128:
                real, imag = real * turn_c + imag * turn_s, imag * turn_c - real * turn_s
        kept = (2 * m < counts) & (group8 < 4)
        scale = jnp.where(m == 0, 1.0 / LONS, 1.0 / (2 * LONS))
        even = jnp.where(kept & (m % 2 == 0), scale, 0.0)
        odd = jnp.where(kept & (m % 2 == 1), scale, 0.0)
        back_even[rows_at(TILE * tile), :] = jnp.concatenate([even, even], axis=0)
        back_odd[rows_at(TILE * tile), :] = jnp.concatenate([odd, odd], axis=0)

    def prepare(start, stop):
        @pl.loop(start, stop)
        def _(tile):
            m = wave_rows(SLOTS * tile, 1)
            make_rows(tile, m)
            low = pair_ref[SLOTS * tile + 4]
            last = jnp.where(row8 % 2 == 1, TOTAL - 1 - low, low)
            both = jnp.where(group8 < 4, m, last)
            kept = 2 * both < counts
            even = jnp.where(kept & (both % 2 == 0), 1.0, 0.0)
            odd = jnp.where(kept & (both % 2 == 1), 1.0, 0.0)
            keep_even[rows_at(TILE * tile), :] = jnp.concatenate([even, even], axis=0).astype(BF16)
            keep_odd[rows_at(TILE * tile), :] = jnp.concatenate([odd, odd], axis=0).astype(BF16)

    def prepare_last():
        @pl.loop(0, WAVES // 4)
        def _(q):
            make_rows(WAVES + q, wave_rows(4 * SLOTS * q + 4, SLOTS))

    lev_send(0, s1, r1)
    prepare(0, 24)
    row = iota((160, 160), 0)
    column = iota((160, 160), 1)
    sel_out[...] = (column == group_row(row, row // 80)).astype(BF16)
    sel_in[...] = (row == group_row(column, column // 80)).astype(BF16)
    all_landed(0, r1)
    s2[...] = dot(mixm[...], r1[...]).astype(BF16)
    lev_send(1, s2, r2)
    prepare(24, 48)
    dr, dc = iota((1024, 256), 0), iota((1024, 256), 1)
    wanted = 16 * (dr // 64) + 8 * ((dr // 2) % 2) + 2 * ((dr // 16) % 4) + dr % 2
    dup[...] = (dc == wanted).astype(BF16)
    all_landed(1, r2)
    leg_copy.wait()

    for s in range(SLOTS):
        low = pair_ref[SLOTS * w + s]
        pieces = []
        corner = None
        for e in range(3):
            pair_chunk = r2[TILE * (3 * s + e) : TILE * (3 * s + e) + TILE, :].astype(F32)
            for half in range(2):
                a = pair_chunk[8 * half : 8 * half + 8]
                r = lane8 + 128 * (2 * e + half)
                first = r < TOTAL - low
                gap = jnp.where(first, r, r - TOTAL + low)
                sign = jnp.where(gap % 2 == 0, 1.0, -1.0)
                t0 = jnp.where(first, a, 0.0)
                t1 = jnp.where(first, 0.0, a)
                quad = jnp.concatenate([t0, t0 * sign, t1, t1 * sign], axis=0)
                if 2 * e + half < 5:
                    pieces.append(quad.astype(BF16))
                else:
                    corner = quad[:, 0:1]
        coefs = jnp.concatenate(pieces, axis=1)
        last_row = leg_v[s, TOTAL : TOTAL + 1, :].astype(F32)
        total = dot(coefs, leg_v[s, 0:TOTAL, :]) + corner * last_row
        fb[32 * s : 32 * s + 32, :] = total.astype(BF16)

    f = dot(sel_out[...], fb[...])
    lane = iota((32, 768), 1) // BAND % 5
    blank = jnp.zeros((32, 128), F32)
    shifted = []
    for g in range(5):
        part = jnp.concatenate([f[16 * g : 16 * g + 16], f[80 + 16 * g : 96 + 16 * g]], axis=0)
        wide = jnp.concatenate([part, blank], axis=1)
        shifted.append(wide if g == 0 else pltpu.roll(wide, BAND * g, axis=1))
    for beta in range(5):
        merged = shifted[0]
        for g in range(1, 5):
            merged = jnp.where(lane == (g + beta) % 5, shifted[g], merged)
        hs[32 * beta : 32 * beta + 32, :] = merged

    own_north = jnp.where(north, w, WAVES - 1 - w)

    def wave_send(phase, source, target, d):
        pltpu.make_async_remote_copy(
            src_ref=source.at[rows_at(TILE * d)],
            dst_ref=target.at[rows_at(TILE * w)],
            send_sem=send_sem.at[phase],
            recv_sem=recv_sem.at[phase],
            device_id={"wave": d},
            device_id_type=MESH,
        ).start()

    def keep_own(phase, source, target):
        pltpu.make_async_copy(
            source.at[rows_at(TILE * w)], target.at[rows_at(TILE * w)], recv_sem.at[phase]
        ).start()

    def window_of(b):
        start = BAND * b
        aligned = (start // 128) * 128
        return pl.ds(pl.multiple_of(aligned, 128), 256), start - aligned

    def cut(b):
        lanes, offset = window_of(b)
        window = hs[rows_at(32 * lax.rem(b, 5), 32), lanes]
        message = pltpu.roll(window, lax.rem(256 - offset, 256), axis=1)[:, 0:128].astype(BF16)
        s3[rows_at(TILE * b), :] = message[0:16]
        s3[rows_at(TILE * (WAVES - 1 - b)), :] = message[16:32]

    @pl.loop(1, WAVES // 2)
    def _(i):
        b = lax.rem(own_north + i, WAVES // 2)
        cut(b)
        wave_send(2, s3, r3, b)
        wave_send(2, s3, r3, WAVES - 1 - b)

    cut(own_north)
    wave_send(2, s3, r3, WAVES - 1 - w)
    keep_own(2, s3, r3)

    prepare(48, WAVES)
    prepare_last()
    wind_copy.wait()

    @pl.loop(0, BAND // 2)
    def _(q):
        wind_f[q, 0:4, :] = wind_v[2 * q].astype(F32)
        wind_f[q, 4:8, :] = wind_v[2 * q + 1].astype(F32)

    all_landed(2, r3)

    qi = iota((160, 128), 0)
    ql = iota((160, 128), 1)
    lat_row = (qi % 80) // 4
    node = jnp.where(north, lat_row, BAND - 1 - lat_row)
    group = jnp.where(qi < 80, qi % 4, 4)
    gather = (ql == BAND * group + node).astype(BF16)
    level_match = iota((80, 1024), 0) % 4 == (iota((80, 1024), 1) // 4) % 4
    for half, keep in enumerate((keep_even, keep_odd)):
        y = dot_nt(gather, r3[...] * keep[...])
        xt[80 * half : 80 * half + 80, 0:1024] = y[0:80].astype(BF16)
        single = jnp.where(level_match, y[80:160], 0.0).astype(BF16)
        xt[80 * half : 80 * half + 80, 1024:COLS] = dot(single, dup[...]).astype(BF16)

    si = iota((256, 160), 0)
    sj = iota((256, 160), 1)
    half_row = si // 128
    lane_row = si % 128
    lat_nat = jnp.where(north, lane_row % BAND, BAND - 1 - lane_row % BAND)
    wanted_col = 80 * half_row + 4 * lat_nat + lane_row // BAND
    scatter = ((sj == wanted_col) & (lane_row < 80)).astype(BF16)

    @pl.loop(0, HALF // 256)
    def _(j):
        low = pl.ds(pl.multiple_of(256 * j, 256), 256)
        high = pl.ds(pl.multiple_of(HALF + 256 * j, 256), 256)
        g = dot(xt[...], basis[:, low])
        even, odd = g[0:80], g[80:160]
        near = (even + odd).astype(BF16).astype(F32) * wind_f[:, :, low].reshape(80, 256)
        far = (even - odd).astype(BF16).astype(F32) * wind_f[:, :, high].reshape(80, 256)
        ff[0:80, :] = (near + far).astype(BF16)
        ff[80:160, :] = (near - far).astype(BF16)
        fp[:, low] = dot(scatter, ff[...]).astype(BF16)

    @pl.loop(0, COLS // 256)
    def _(j):
        rows = pl.ds(pl.multiple_of(256 * j, 256), 256)
        product = dot_nt(basis[rows, :], fp[...])
        bk[rows, :] = (
            product[:, 0:128] * back_even[rows, :] + product[:, 128:256] * back_odd[rows, :]
        ).astype(BF16)

    zi, zl = iota((1024, 128), 0), iota((1024, 128), 1)
    own_level = (zl // BAND) == (zi // 4) % 4
    fold_r, fold_c = iota((128, 128), 0), iota((128, 128), 1)
    fold = ((fold_c == 80 + fold_r % BAND) & (fold_r < 80)).astype(BF16)
    last_rows = jnp.where(own_level, dot(dup[...], bk[1024:COLS, :]), 0.0).astype(BF16)
    s5[...] = (bk[0:1024, :].astype(F32) + dot(last_rows, fold)).astype(BF16)

    @pl.loop(1, WAVES)
    def _(i):
        wave_send(3, s5, r5, lax.rem(w + i, WAVES))

    keep_own(3, s5, r5)
    hs[...] = jnp.zeros_like(hs)
    all_landed(3, r5)

    empty = jnp.zeros((32, 128), F32)

    @pl.loop(0, WAVES // 2)
    def _(b):
        lanes, offset = window_of(b)
        upper = r5[rows_at(TILE * b), :].astype(F32)
        lower = r5[rows_at(TILE * (WAVES - 1 - b)), :].astype(F32)
        folded = jnp.concatenate([upper + lower, upper - lower], axis=0)
        placed = pltpu.roll(jnp.concatenate([folded, empty], axis=1), offset, axis=1)
        hs[rows_at(32 * lax.rem(b, 5), 32), lanes] += placed

    weights = qw_ref[...]
    for g in range(5):
        merged = hs[0:32, :]
        for beta in range(1, 5):
            merged = jnp.where(lane == (g + beta) % 5, hs[32 * beta : 32 * beta + 32, :], merged)
        if g:
            merged = pltpu.roll(merged, 768 - BAND * g, axis=1)
        merged = (merged[:, 0:TOTAL] * weights).astype(BF16)
        fb[16 * g : 16 * g + 16, :] = merged[0:16]
        fb[80 + 16 * g : 96 + 16 * g, :] = merged[16:32]

    folded_rows = dot(sel_in[...], fb[...]).astype(BF16)
    r_all = iota((8, TOTAL + 1), 1)
    for s in range(SLOTS):
        low = pair_ref[SLOTS * w + s]
        first = r_all < TOTAL - low
        gap = jnp.where(first, r_all, r_all - TOTAL + low)
        odd = gap % 2 == 1
        o = dot_nt(folded_rows[32 * s : 32 * s + 32], leg_v[s])
        result = jnp.where(
            first, jnp.where(odd, o[8:16], o[0:8]), jnp.where(odd, o[24:32], o[16:24])
        )
        out_ref[s, 0] = result[0:4]
        out_ref[s, 1] = result[4:8]

    all_sent(0, s1)
    all_sent(1, s2)
    all_sent(2, s3)
    all_sent(3, s5)


def shards(spectral, legendre, quad_weights, pair_order, lon_counts, vertical, wind_field):
    vmem = pl.BlockSpec(memory_space=pltpu.VMEM)
    smem = pl.BlockSpec(memory_space=pltpu.SMEM)
    hbm = pl.BlockSpec(memory_space=pl.ANY)
    message = pltpu.VMEM((TILE * WAVES, 128), BF16)
    tiles = pltpu.VMEM((TILE * LEVS, 128), BF16)
    return pl.pallas_call(
        kernel,
        out_shape=jax.ShapeDtypeStruct(spectral.shape, F32),
        in_specs=[vmem, hbm, vmem, smem, smem, vmem, hbm],
        out_specs=vmem,
        scratch_shapes=[
            pltpu.VMEM(legendre.shape, BF16),
            pltpu.VMEM(wind_field.shape, BF16),
            pltpu.VMEM((BAND // 2, 8, LONS), F32),
            pltpu.VMEM((256, 256), BF16),
            pltpu.VMEM((LEVS, TILE, 128), F32),
            tiles,
            tiles,
            tiles,
            tiles,
            pltpu.VMEM((COLS, HALF), BF16),
            message,
            message,
            pltpu.VMEM((COLS, 128), F32),
            pltpu.VMEM((COLS, 128), F32),
            pltpu.VMEM((160, TOTAL), BF16),
            pltpu.VMEM((160, 768), F32),
            pltpu.VMEM((160, 160), BF16),
            pltpu.VMEM((160, 160), BF16),
            message,
            message,
            pltpu.VMEM((160, COLS), BF16),
            pltpu.VMEM((160, 256), BF16),
            pltpu.VMEM((256, HALF), BF16),
            pltpu.VMEM((COLS, 128), BF16),
            message,
            message,
            pltpu.VMEM((1024, 256), BF16),
            pltpu.SemaphoreType.DMA((2,)),
            pltpu.SemaphoreType.DMA((4,)),
            pltpu.SemaphoreType.DMA((4,)),
        ],
        compiler_params=pltpu.CompilerParams(
            collective_id=0, has_side_effects=True, vmem_limit_bytes=50 * 1024 * 1024
        ),
    )(
        spectral,
        legendre,
        quad_weights.reshape(1, TOTAL),
        pair_order,
        lon_counts,
        vertical,
        wind_field,
    )


def solution(mesh):
    return jax.shard_map(
        shards,
        mesh=mesh,
        in_specs=(
            P("wave", None, "lev", None),
            P("wave", None, None),
            P(),
            P(),
            P(),
            P(),
            P("wave", "lev", None),
        ),
        out_specs=P("wave", None, "lev", None),
        check_vma=False,
    )
```

```python
import math

import jax
import jax.numpy as jnp
from jax import lax
from jax.experimental import pallas as pl
from jax.experimental.pallas import tpu as pltpu
from jax.sharding import PartitionSpec as P

MESH = pl.DeviceIdType.MESH
F32 = jnp.float32
BF16 = jnp.bfloat16

WAVES = 64
LEVS = 16
SLOTS = 5
LEVELS = 4
TOTAL = 640
BAND = 20
LONS = 2560
HALF = LONS // 2
TILE = 16
MIXERS = 13
GROUPS = 4
GROUP_ROWS = TILE * WAVES // GROUPS
COLS = 2 * SLOTS * 2 * WAVES


def dot(a, b):
    return jnp.dot(a, b, preferred_element_type=F32)


def dot_nt(a, b):
    return lax.dot_general(a, b, (((1,), (1,)), ((), ())), preferred_element_type=F32)


def iota(shape, dim):
    return lax.broadcasted_iota(jnp.int32, shape, dim)


def rows_at(start, size=TILE):
    return pl.ds(pl.multiple_of(start, TILE), size)


def half_angle(phase):
    wrapped = phase - float(LONS) * jnp.floor(phase * (1.0 / LONS) + 0.5)
    u = wrapped * (math.pi / LONS)
    q = u * u
    sine = u * (
        1.0
        + q * (-1 / 6 + q * (1 / 120 + q * (-1 / 5040 + q * (1 / 362880 + q * (-1 / 39916800)))))
    )
    cosine = 1.0 + q * (
        -1 / 2
        + q * (1 / 24 + q * (-1 / 720 + q * (1 / 40320 + q * (-1 / 3628800 + q * (1 / 479001600)))))
    )
    return 1.0 - 2.0 * sine * sine, 2.0 * sine * cosine


def group_row(row, half):
    g, rho = (row - 80 * half) // TILE, row % TILE
    last = g == 4
    s = jnp.where(last, 4, (rho // 2) % 4)
    t = rho % 2
    c = jnp.where(last, (rho // 2) % 2, rho // 8)
    level = jnp.where(last, rho // 4, g)
    return 32 * s + 16 * t + 8 * half + 4 * c + level


def kernel(
    spec_hbm,
    leg_hbm,
    qw_hbm,
    pair_hbm,
    cnt_hbm,
    vert_hbm,
    wind_hbm,
    out_ref,
    spec_ref,
    qw_ref,
    pair_ref,
    cnt_ref,
    vert_ref,
    leg_v,
    wind_v,
    wind_f,
    mixm,
    s1f,
    s1,
    r1,
    s2,
    r2,
    basis,
    keep_even,
    keep_odd,
    back_even,
    back_odd,
    fb,
    hs,
    sel_out,
    sel_in,
    s3,
    r3,
    xt,
    acc,
    ff,
    fp,
    s5,
    r5,
    dup,
    dup_one,
    ready,
    local_sem,
    send_sem,
    recv_sem,
):
    w = lax.axis_index("wave")
    v = lax.axis_index("lev")
    north = w < WAVES // 2

    small = (
        (spec_hbm, spec_ref),
        (vert_hbm, vert_ref),
        (pair_hbm, pair_ref),
        (cnt_hbm, cnt_ref),
        (qw_hbm, qw_ref),
    )
    loads = [
        pltpu.make_async_copy(source, target, local_sem.at[2 + i])
        for i, (source, target) in enumerate(small)
    ]
    for copy in loads:
        copy.start()

    barrier = pltpu.get_barrier_semaphore()

    @pl.loop(1, LEVS)
    def _(i):
        pl.semaphore_signal(barrier, 1, device_id={"lev": lax.rem(v + i, LEVS)}, device_id_type=MESH)

    major, minor = w // 8, w % 8

    @pl.loop(1, 8)
    def _(i):
        across = 8 * lax.rem(major + i, 8) + minor
        pl.semaphore_signal(barrier, 1, device_id={"wave": across}, device_id_type=MESH)
        along = 8 * major + lax.rem(minor + i, 8)
        pl.semaphore_signal(barrier, 1, device_id={"wave": along}, device_id_type=MESH)

    for copy in loads:
        copy.wait()
    leg_copy = pltpu.make_async_copy(leg_hbm, leg_v, local_sem.at[0])
    leg_copy.start()
    wind_copy = pltpu.make_async_copy(wind_hbm, wind_v, local_sem.at[1])
    wind_copy.start()

    first_lane = iota((LEVELS, 128), 1)

    @pl.loop(0, SLOTS)
    def _(s):
        for c in range(2):
            for chunk in range(5):
                piece = spec_ref[s, c, :, 128 * chunk : 128 * chunk + 128].astype(F32)
                s1f[5 * s + chunk, 4 * c : 4 * c + 4, :] = piece

    for c in range(2):
        piece = jnp.zeros((LEVELS, 128), F32)
        for s in range(SLOTS):
            column = spec_ref[s, c, :, TOTAL : TOTAL + 1].astype(F32)
            piece = jnp.where(first_lane == s, jnp.broadcast_to(column, (LEVELS, 128)), piece)
        s1f[25, 4 * c : 4 * c + 4, :] = piece
    s1[...] = s1f[...].reshape(TILE * MIXERS, 128).astype(BF16)

    pl.semaphore_wait(barrier, LEVS - 1 + 14)

    def lev_send(phase, source, target, d, here, there):
        pltpu.make_async_remote_copy(
            src_ref=source.at[rows_at(TILE * here)],
            dst_ref=target.at[rows_at(TILE * there)],
            send_sem=send_sem.at[phase],
            recv_sem=recv_sem.at[phase],
            device_id={"lev": d},
            device_id_type=MESH,
        ).start()

    def keep_own(phase, source, target, here, there):
        pltpu.make_async_copy(
            source.at[rows_at(TILE * here)], target.at[rows_at(TILE * there)], recv_sem.at[phase]
        ).start()

    def landed(phase, part):
        pltpu.make_async_copy(part, part, recv_sem.at[phase]).wait()

    def sent(phase, part):
        pltpu.make_async_copy(part, part, send_sem.at[phase]).wait()

    lane8 = iota((8, 128), 1)
    row8 = iota((8, 128), 0)
    group8 = lane8 // BAND
    lat_of = lane8 % BAND
    counts = jnp.zeros((8, 128), jnp.int32)
    for jj in range(BAND):
        lat = jnp.where(north, BAND * w + jj, BAND * w + BAND - 1 - jj)
        counts = jnp.where(lat_of == jj, cnt_ref[lat], counts)
    counts = jnp.where(group8 < 5, counts, 0)

    def wave_rows(first, stride):
        m = jnp.zeros((8, 128), jnp.int32)
        for i in range(4):
            m = jnp.where(row8 // 2 == i, pair_ref[first + stride * i], m)
        return jnp.where(row8 % 2 == 1, TOTAL - 1 - m, m)

    def make_rows(tile, m):
        mf = m.astype(F32)
        factor = jnp.where(m == 0, 1.0, 2.0)
        cos0, sin0 = half_angle(mf * lane8.astype(F32))
        turn_c, turn_s = half_angle(mf * 128.0)
        real, imag = factor * cos0, -factor * sin0
        for a in range(HALF // 128):
            basis[rows_at(TILE * tile), 128 * a : 128 * a + 128] = jnp.concatenate(
                [real, imag], axis=0
            ).astype(BF16)
            if a + 1 < HALF // 128:
                real, imag = real * turn_c + imag * turn_s, imag * turn_c - real * turn_s
        kept = (2 * m < counts) & (group8 < 4)
        scale = jnp.where(m == 0, 1.0 / LONS, 1.0 / (2 * LONS))
        even = jnp.where(kept & (m % 2 == 0), scale, 0.0)
        odd = jnp.where(kept & (m % 2 == 1), scale, 0.0)
        back_even[rows_at(TILE * tile), :] = jnp.concatenate([even, even], axis=0)
        back_odd[rows_at(TILE * tile), :] = jnp.concatenate([odd, odd], axis=0)

    def prepare(start, stop):
        @pl.loop(start, stop)
        def _(tile):
            owner = 4 * lax.rem(tile, TILE) + tile // TILE
            m = wave_rows(SLOTS * owner, 1)
            make_rows(tile, m)
            low = pair_ref[SLOTS * owner + 4]
            last = jnp.where(row8 % 2 == 1, TOTAL - 1 - low, low)
            both = jnp.where(group8 < 4, m, last)
            kept = 2 * both < counts
            even = jnp.where(kept & (both % 2 == 0), 1.0, 0.0)
            odd = jnp.where(kept & (both % 2 == 1), 1.0, 0.0)
            keep_even[rows_at(TILE * tile), :] = jnp.concatenate([even, even], axis=0).astype(BF16)
            keep_odd[rows_at(TILE * tile), :] = jnp.concatenate([odd, odd], axis=0).astype(BF16)

    def prepare_last():
        @pl.loop(0, WAVES // 4)
        def _(q):
            owner = TILE * lax.rem(q, 4) + q // 4
            make_rows(WAVES + q, wave_rows(SLOTS * owner + 4, 4 * SLOTS))

    @pl.loop(0, LEVS)
    def _(i):
        d = lax.rem(v + i, LEVS)

        @pl.when((d < MIXERS) & (d != v))
        def _():
            lev_send(0, s1, r1, d, d, v)

    @pl.when(v < MIXERS)
    def _():
        keep_own(0, s1, r1, v, v)

    pick = (iota((256, 64), 1) == 4 * (iota((256, 64), 0) // 16) + iota((256, 64), 0) % 4).astype(BF16)
    spread = dot_nt(dot(pick, vert_ref[...]).astype(BF16), pick)
    same = (iota((256, 256), 0) // 4) % 4 == (iota((256, 256), 1) // 4) % 4
    mixm[...] = jnp.where(same, spread, 0.0).astype(BF16)

    prepare(0, 24)
    row = iota((160, 160), 0)
    column = iota((160, 160), 1)
    sel_out[...] = (column == group_row(row, row // 80)).astype(BF16)
    sel_in[...] = (row == group_row(column, column // 80)).astype(BF16)

    @pl.when(v < MIXERS)
    def _():
        landed(0, r1)
        s2[...] = dot(mixm[...], r1[...]).astype(BF16)

        @pl.loop(1, LEVS)
        def _(i):
            d = lax.rem(v + i, LEVS)
            lev_send(1, s2, r2, d, d, v)

        keep_own(1, s2, r2, v, v)

    @pl.loop(1, 8)
    def _(i):
        across = 8 * lax.rem(major + i, 8) + minor
        pl.semaphore_signal(ready, 1, device_id={"wave": across}, device_id_type=MESH)

    prepare(24, 48)
    dr, dc = iota((1024, 256), 0), iota((1024, 256), 1)
    wanted = 16 * (dr // 64) + 8 * ((dr // 2) % 2) + 2 * ((dr // 16) % 4) + dr % 2
    dup[...] = (dc == wanted).astype(BF16)
    dup_one[...] = dup[0:256, 0:128]
    landed(1, r2)
    leg_copy.wait()

    for s in range(SLOTS):
        low = pair_ref[SLOTS * w + s]
        pieces = []
        corner = None
        for chunk in range(6):
            if chunk < 5:
                a = r2[40 * s + 8 * chunk : 40 * s + 8 * chunk + 8, :].astype(F32)
            else:
                a = r2[200:208, :].astype(F32)
            r = lane8 + 128 * chunk if chunk < 5 else jnp.full((8, 128), TOTAL, jnp.int32)
            first = r < TOTAL - low
            gap = jnp.where(first, r, r - TOTAL + low)
            sign = jnp.where(gap % 2 == 0, 1.0, -1.0)
            t0 = jnp.where(first, a, 0.0)
            t1 = jnp.where(first, 0.0, a)
            quad = jnp.concatenate([t0, t0 * sign, t1, t1 * sign], axis=0)
            if chunk < 5:
                pieces.append(quad.astype(BF16))
            else:
                corner = quad[:, s : s + 1]
        coefs = jnp.concatenate(pieces, axis=1)
        last_row = leg_v[s, TOTAL : TOTAL + 1, :].astype(F32)
        total = dot(coefs, leg_v[s, 0:TOTAL, :]) + corner * last_row
        fb[32 * s : 32 * s + 32, :] = total.astype(BF16)

    f = dot(sel_out[...], fb[...])
    lane = iota((32, 768), 1) // BAND % 5
    blank = jnp.zeros((32, 128), F32)
    shifted = []
    for g in range(5):
        part = jnp.concatenate([f[16 * g : 16 * g + 16], f[80 + 16 * g : 96 + 16 * g]], axis=0)
        wide = jnp.concatenate([part, blank], axis=1)
        shifted.append(wide if g == 0 else pltpu.roll(wide, BAND * g, axis=1))
    for beta in range(5):
        merged = shifted[0]
        for g in range(1, 5):
            merged = jnp.where(lane == (g + beta) % 5, shifted[g], merged)
        hs[32 * beta : 32 * beta + 32, :] = merged

    def slot_of(device):
        return TILE * lax.rem(device, GROUPS) + device // GROUPS

    group = lax.rem(w, GROUPS)
    own_slot = slot_of(w)

    def wave_send(phase, source, target, k, d):
        pltpu.make_async_remote_copy(
            src_ref=source.at[rows_at(TILE * slot_of(d))],
            dst_ref=target.at[rows_at(TILE * own_slot)],
            send_sem=send_sem.at[phase],
            recv_sem=recv_sem.at[2 + GROUPS * (phase - 2) + k],
            device_id={"wave": d},
            device_id_type=MESH,
        ).start()

    def window_of(b):
        start = BAND * b
        aligned = (start // 128) * 128
        return pl.ds(pl.multiple_of(aligned, 128), 256), start - aligned

    def mirror(band):
        upper = band < WAVES // 2
        return jnp.where(upper, band, WAVES - 1 - band), jnp.where(upper, 0, TILE), upper

    def cut(d):
        b, south, _ = mirror(d)
        lanes, offset = window_of(b)
        window = hs[rows_at(32 * lax.rem(b, 5) + south), lanes]
        message = pltpu.roll(window, lax.rem(256 - offset, 256), axis=1)[:, 0:128].astype(BF16)
        s3[rows_at(TILE * slot_of(d)), :] = message

    def target_of(k, j):
        return lax.rem(group + k, GROUPS) + GROUPS * lax.rem(w // GROUPS + j, TILE)

    pl.semaphore_wait(ready, 7)
    for k in range(GROUPS):

        @pl.loop(0, TILE, unroll=8)
        def _(j):
            cut(target_of(k, j))

        if k == 0:
            keep_own(2, s3, r3, own_slot, own_slot)

        @pl.loop(0 if k else 1, TILE)
        def _(j):
            wave_send(2, s3, r3, k, target_of(k, j))

    prepare(48, WAVES)
    prepare_last()
    wind_copy.wait()

    @pl.loop(0, BAND // 2)
    def _(q):
        wind_f[q, 0:4, :] = wind_v[2 * q].astype(F32)
        wind_f[q, 4:8, :] = wind_v[2 * q + 1].astype(F32)

    qi = iota((160, 128), 0)
    ql = iota((160, 128), 1)
    lat_row = (qi % 80) // 4
    node = jnp.where(north, lat_row, BAND - 1 - lat_row)
    column_of = jnp.where(qi < 80, qi % 4, 4)
    gather = (ql == BAND * column_of + node).astype(BF16)
    level_match = iota((80, 256), 0) % 4 == (iota((80, 256), 1) // 4) % 4
    singles = [jnp.zeros((80, 256), F32)] * 2
    for k in range(GROUPS):
        block = pl.ds(pl.multiple_of(GROUP_ROWS * lax.rem(group - k + GROUPS, GROUPS), GROUP_ROWS), GROUP_ROWS)
        landed(2 + k, r3.at[block])
        for half, keep in enumerate((keep_even, keep_odd)):
            y = dot_nt(gather, r3[block, :] * keep[block, :])
            xt[80 * half : 80 * half + 80, 0:256] = y[0:80].astype(BF16)
            single = jnp.where(level_match, y[80:160], 0.0).astype(BF16)
            singles[half] = singles[half] + dot(single, dup[block, :])
        if k + 1 < GROUPS:

            for j in range(HALF // 256):
                low = pl.ds(256 * j, 256)
                term = dot(xt[:, 0:256], basis[block, low])
                acc[:, low] = acc[:, low] + term if k else term

    for half in range(2):
        xt[80 * half : 80 * half + 80, 256:512] = singles[half].astype(BF16)

    si = iota((256, 160), 0)
    sj = iota((256, 160), 1)
    half_row = si // 128
    lane_row = si % 128
    lat_nat = jnp.where(north, lane_row % BAND, BAND - 1 - lane_row % BAND)
    wanted_col = 80 * half_row + 4 * lat_nat + lane_row // BAND
    scatter = ((sj == wanted_col) & (lane_row < 80)).astype(BF16)

    for j in range(HALF // 256):
        low = pl.ds(256 * j, 256)
        high = pl.ds(HALF + 256 * j, 256)
        g = (
            acc[:, low]
            + dot(xt[:, 0:256], basis[block, low])
            + dot(xt[:, 256:512], basis[1024:COLS, low])
        )
        even, odd = g[0:80], g[80:160]
        near = (even + odd).astype(BF16).astype(F32) * wind_f[:, :, low].reshape(80, 256)
        far = (even - odd).astype(BF16).astype(F32) * wind_f[:, :, high].reshape(80, 256)
        ff[0:80, :] = (near + far).astype(BF16)
        ff[80:160, :] = (near - far).astype(BF16)
        fp[:, low] = dot(scatter, ff[...]).astype(BF16)

    zi, zl = iota((256, 128), 0), iota((256, 128), 1)
    own_level = (zl // BAND) == (zi // 4) % 4
    fold_r, fold_c = iota((128, 128), 0), iota((128, 128), 1)
    fold = ((fold_c == 80 + fold_r % BAND) & (fold_r < 80)).astype(BF16)

    def spectral_rows(rows):
        product = dot_nt(basis[rows, :], fp[...])
        return product[:, 0:128] * back_even[rows, :] + product[:, 128:256] * back_odd[rows, :]

    for k in range(GROUPS):
        target_group = lax.rem(group + k, GROUPS)
        block = pl.ds(pl.multiple_of(GROUP_ROWS * target_group, GROUP_ROWS), GROUP_ROWS)
        main = spectral_rows(block).astype(BF16).astype(F32)
        single = spectral_rows(pl.ds(pl.multiple_of(1024 + 64 * target_group, 64), 64)).astype(BF16)
        spread_rows = jnp.where(own_level, dot(dup_one[:, 0:64], single), 0.0).astype(BF16)
        s5[block, :] = (main + dot(spread_rows, fold)).astype(BF16)
        if k == 0:
            keep_own(6, s5, r5, own_slot, own_slot)

        @pl.loop(0 if k else 1, TILE)
        def _(j):
            wave_send(3, s5, r5, k, target_of(k, j))

    hs[...] = jnp.zeros_like(hs)
    empty = jnp.zeros((TILE, 128), F32)
    for k in range(GROUPS):
        source_group = lax.rem(group - k + GROUPS, GROUPS)
        landed(6 + k, r5.at[rows_at(GROUP_ROWS * source_group, GROUP_ROWS)])

        @pl.loop(0, TILE, unroll=4)
        def _(j):
            b, _, upper = mirror(GROUPS * j + source_group)
            lanes, offset = window_of(b)
            message = r5[rows_at(GROUP_ROWS * source_group + TILE * j), :].astype(F32)
            placed = pltpu.roll(jnp.concatenate([message, empty], axis=1), offset, axis=1)
            at = 32 * lax.rem(b, 5)
            hs[rows_at(at), lanes] += placed
            hs[rows_at(at + TILE), lanes] += placed * jnp.where(upper, 1.0, -1.0)

    weights = qw_ref[...].reshape(1, TOTAL)
    for g in range(5):
        merged = hs[0:32, :]
        for beta in range(1, 5):
            merged = jnp.where(lane == (g + beta) % 5, hs[32 * beta : 32 * beta + 32, :], merged)
        if g:
            merged = pltpu.roll(merged, 768 - BAND * g, axis=1)
        merged = (merged[:, 0:TOTAL] * weights).astype(BF16)
        fb[16 * g : 16 * g + 16, :] = merged[0:16]
        fb[80 + 16 * g : 96 + 16 * g, :] = merged[16:32]

    folded_rows = dot(sel_in[...], fb[...]).astype(BF16)
    r_all = iota((8, TOTAL + 1), 1)
    for s in range(SLOTS):
        low = pair_ref[SLOTS * w + s]
        first = r_all < TOTAL - low
        gap = jnp.where(first, r_all, r_all - TOTAL + low)
        odd = gap % 2 == 1
        o = dot_nt(folded_rows[32 * s : 32 * s + 32], leg_v[s])
        result = jnp.where(
            first, jnp.where(odd, o[8:16], o[0:8]), jnp.where(odd, o[24:32], o[16:24])
        )
        out_ref[s, 0] = result[0:4]
        out_ref[s, 1] = result[4:8]

    @pl.when(v < MIXERS)
    def _():
        sent(0, s1.at[pl.ds(0, TILE * (MIXERS - 1))])
        sent(1, s2.at[pl.ds(0, TILE * (LEVS - 1))])

    @pl.when(v >= MIXERS)
    def _():
        sent(0, s1)

    sent(2, s3.at[pl.ds(0, TILE * (WAVES - 1))])
    sent(3, s5.at[pl.ds(0, TILE * (WAVES - 1))])


def shards(spectral, legendre, quad_weights, pair_order, lon_counts, vertical, wind_field):
    vmem = pl.BlockSpec(memory_space=pltpu.VMEM)
    hbm = pl.BlockSpec(memory_space=pltpu.HBM)
    message = pltpu.VMEM((TILE * WAVES, 128), BF16)
    tiles = pltpu.VMEM((TILE * LEVS, 128), BF16)
    return pl.pallas_call(
        kernel,
        out_shape=jax.ShapeDtypeStruct(spectral.shape, F32),
        in_specs=[hbm] * 7,
        out_specs=vmem,
        scratch_shapes=[
            pltpu.VMEM(spectral.shape, BF16),
            pltpu.VMEM(quad_weights.shape, F32),
            pltpu.SMEM(pair_order.shape, jnp.int32),
            pltpu.SMEM(lon_counts.shape, jnp.int32),
            pltpu.VMEM(vertical.shape, BF16),
            pltpu.VMEM(legendre.shape, BF16),
            pltpu.VMEM(wind_field.shape, BF16),
            pltpu.VMEM((BAND // 2, 8, LONS), F32),
            pltpu.VMEM((256, 256), BF16),
            pltpu.VMEM((2 * MIXERS, 8, 128), F32),
            pltpu.VMEM((TILE * MIXERS, 128), BF16),
            tiles,
            tiles,
            pltpu.VMEM((TILE * MIXERS, 128), BF16),
            pltpu.VMEM((COLS, HALF), BF16),
            message,
            message,
            pltpu.VMEM((COLS, 128), F32),
            pltpu.VMEM((COLS, 128), F32),
            pltpu.VMEM((160, TOTAL), BF16),
            pltpu.VMEM((160, 768), F32),
            pltpu.VMEM((160, 160), BF16),
            pltpu.VMEM((160, 160), BF16),
            message,
            message,
            pltpu.VMEM((160, 512), BF16),
            pltpu.VMEM((160, HALF), F32),
            pltpu.VMEM((160, 256), BF16),
            pltpu.VMEM((256, HALF), BF16),
            message,
            message,
            pltpu.VMEM((1024, 256), BF16),
            pltpu.VMEM((256, 128), BF16),
            pltpu.SemaphoreType.REGULAR,
            pltpu.SemaphoreType.DMA((7,)),
            pltpu.SemaphoreType.DMA((4,)),
            pltpu.SemaphoreType.DMA((10,)),
        ],
        compiler_params=pltpu.CompilerParams(
            collective_id=0, has_side_effects=True, vmem_limit_bytes=63 * 1024 * 1024
        ),
    )(
        spectral,
        legendre,
        quad_weights,
        pair_order,
        lon_counts,
        vertical,
        wind_field,
    )


def solution(mesh):
    return jax.shard_map(
        shards,
        mesh=mesh,
        in_specs=(
            P("wave", None, "lev", None),
            P("wave", None, None),
            P(),
            P(),
            P(),
            P(),
            P("wave", "lev", None),
        ),
        out_specs=P("wave", None, "lev", None),
        check_vma=False,
    )
```

```python
import math

import jax
import jax.numpy as jnp
from jax import lax
from jax.experimental import pallas as pl
from jax.experimental.pallas import tpu as pltpu
from jax.sharding import PartitionSpec as P

MESH = pl.DeviceIdType.MESH
F32 = jnp.float32
BF16 = jnp.bfloat16

WAVES = 64
LEVS = 16
SLOTS = 5
LEVELS = 4
TOTAL = 640
BAND = 20
LONS = 2560
HALF = LONS // 2
TILE = 16
MIXERS = 13
GROUPS = 4
ORDER = (2, 1, 3, 0)
GROUP_ROWS = TILE * WAVES // GROUPS
COLS = 2 * SLOTS * 2 * WAVES


def dot(a, b):
    return jnp.dot(a, b, preferred_element_type=F32)


def dot_nt(a, b):
    return lax.dot_general(a, b, (((1,), (1,)), ((), ())), preferred_element_type=F32)


def iota(shape, dim):
    return lax.broadcasted_iota(jnp.int32, shape, dim)


def rows_at(start, size=TILE):
    return pl.ds(pl.multiple_of(start, TILE), size)


def half_angle(phase):
    wrapped = phase - float(LONS) * jnp.floor(phase * (1.0 / LONS) + 0.5)
    u = wrapped * (math.pi / LONS)
    q = u * u
    sine = u * (
        1.0
        + q * (-1 / 6 + q * (1 / 120 + q * (-1 / 5040 + q * (1 / 362880 + q * (-1 / 39916800)))))
    )
    cosine = 1.0 + q * (
        -1 / 2
        + q * (1 / 24 + q * (-1 / 720 + q * (1 / 40320 + q * (-1 / 3628800 + q * (1 / 479001600)))))
    )
    return 1.0 - 2.0 * sine * sine, 2.0 * sine * cosine


def group_row(row, half):
    g, rho = (row - 80 * half) // TILE, row % TILE
    last = g == 4
    s = jnp.where(last, 4, (rho // 2) % 4)
    t = rho % 2
    c = jnp.where(last, (rho // 2) % 2, rho // 8)
    level = jnp.where(last, rho // 4, g)
    return 32 * s + 16 * t + 8 * half + 4 * c + level


def kernel(
    spec_hbm,
    leg_hbm,
    qw_hbm,
    pair_hbm,
    cnt_hbm,
    vert_hbm,
    wind_hbm,
    out_ref,
    spec_ref,
    qw_ref,
    pair_ref,
    cnt_ref,
    vert_ref,
    leg_v,
    wind_v,
    wind_f,
    mixm,
    s1f,
    s1,
    r1,
    s2,
    r2,
    basis,
    keep_even,
    keep_odd,
    back_even,
    back_odd,
    fb,
    hs,
    sel_out,
    sel_in,
    s3,
    r3,
    xt,
    acc,
    ff,
    fp,
    s5,
    r5,
    dup,
    dup_one,
    ready,
    local_sem,
    send_sem,
    recv_sem,
):
    w = lax.axis_index("wave")
    v = lax.axis_index("lev")
    north = w < WAVES // 2

    small = (
        (spec_hbm, spec_ref),
        (vert_hbm, vert_ref),
        (pair_hbm, pair_ref),
        (cnt_hbm, cnt_ref),
        (qw_hbm, qw_ref),
    )
    loads = [
        pltpu.make_async_copy(source, target, local_sem.at[2 + i])
        for i, (source, target) in enumerate(small)
    ]
    for copy in loads:
        copy.start()

    barrier = pltpu.get_barrier_semaphore()

    @pl.loop(1, LEVS)
    def _(i):
        pl.semaphore_signal(barrier, 1, device_id={"lev": lax.rem(v + i, LEVS)}, device_id_type=MESH)

    major, minor = w // 8, w % 8

    @pl.loop(1, 8)
    def _(i):
        across = 8 * lax.rem(major + i, 8) + minor
        pl.semaphore_signal(barrier, 1, device_id={"wave": across}, device_id_type=MESH)
        along = 8 * major + lax.rem(minor + i, 8)
        pl.semaphore_signal(barrier, 1, device_id={"wave": along}, device_id_type=MESH)

    for copy in loads:
        copy.wait()
    leg_copy = pltpu.make_async_copy(leg_hbm, leg_v, local_sem.at[0])
    leg_copy.start()
    wind_copy = pltpu.make_async_copy(wind_hbm, wind_v, local_sem.at[1])
    wind_copy.start()

    first_lane = iota((LEVELS, 128), 1)

    @pl.loop(0, SLOTS)
    def _(s):
        for c in range(2):
            for chunk in range(5):
                piece = spec_ref[s, c, :, 128 * chunk : 128 * chunk + 128].astype(F32)
                s1f[5 * s + chunk, 4 * c : 4 * c + 4, :] = piece

    for c in range(2):
        piece = jnp.zeros((LEVELS, 128), F32)
        for s in range(SLOTS):
            column = spec_ref[s, c, :, TOTAL : TOTAL + 1].astype(F32)
            piece = jnp.where(first_lane == s, jnp.broadcast_to(column, (LEVELS, 128)), piece)
        s1f[25, 4 * c : 4 * c + 4, :] = piece
    s1[...] = s1f[...].reshape(TILE * MIXERS, 128).astype(BF16)

    pl.semaphore_wait(barrier, LEVS - 1 + 14)

    def far_first(i):
        return 4 + ((i + 1) // 2) * (1 - 2 * lax.rem(i, 2))

    def lev_target(i):
        return 2 * lax.rem(v // 2 + far_first(i // 2), 8) + lax.rem(v + i + 1, 2)

    def lev_send(phase, source, target, d, here, there):
        pltpu.make_async_remote_copy(
            src_ref=source.at[rows_at(TILE * here)],
            dst_ref=target.at[rows_at(TILE * there)],
            send_sem=send_sem.at[phase],
            recv_sem=recv_sem.at[phase],
            device_id={"lev": d},
            device_id_type=MESH,
        ).start()

    def keep_own(phase, source, target, here, there):
        pltpu.make_async_copy(
            source.at[rows_at(TILE * here)], target.at[rows_at(TILE * there)], recv_sem.at[phase]
        ).start()

    def landed(phase, part):
        pltpu.make_async_copy(part, part, recv_sem.at[phase]).wait()

    def sent(phase, part):
        pltpu.make_async_copy(part, part, send_sem.at[phase]).wait()

    lane8 = iota((8, 128), 1)
    row8 = iota((8, 128), 0)
    group8 = lane8 // BAND
    lat_of = lane8 % BAND
    counts = jnp.zeros((8, 128), jnp.int32)
    for jj in range(BAND):
        lat = jnp.where(north, BAND * w + jj, BAND * w + BAND - 1 - jj)
        counts = jnp.where(lat_of == jj, cnt_ref[lat], counts)
    counts = jnp.where(group8 < 5, counts, 0)

    def wave_rows(first, stride):
        m = jnp.zeros((8, 128), jnp.int32)
        for i in range(4):
            m = jnp.where(row8 // 2 == i, pair_ref[first + stride * i], m)
        return jnp.where(row8 % 2 == 1, TOTAL - 1 - m, m)

    def make_rows(tile, m):
        mf = m.astype(F32)
        factor = jnp.where(m == 0, 1.0, 2.0)
        cos0, sin0 = half_angle(mf * lane8.astype(F32))
        turn_c, turn_s = half_angle(mf * 128.0)
        real, imag = factor * cos0, -factor * sin0
        for a in range(HALF // 128):
            basis[rows_at(TILE * tile), 128 * a : 128 * a + 128] = jnp.concatenate(
                [real, imag], axis=0
            ).astype(BF16)
            if a + 1 < HALF // 128:
                real, imag = real * turn_c + imag * turn_s, imag * turn_c - real * turn_s
        kept = (2 * m < counts) & (group8 < 4)
        scale = jnp.where(m == 0, 1.0 / LONS, 1.0 / (2 * LONS))
        even = jnp.where(kept & (m % 2 == 0), scale, 0.0)
        odd = jnp.where(kept & (m % 2 == 1), scale, 0.0)
        back_even[rows_at(TILE * tile), :] = jnp.concatenate([even, even], axis=0)
        back_odd[rows_at(TILE * tile), :] = jnp.concatenate([odd, odd], axis=0)

    def prepare(start, stop):
        @pl.loop(start, stop)
        def _(tile):
            m = wave_rows(SLOTS * tile, 1)
            make_rows(tile, m)
            low = pair_ref[SLOTS * tile + 4]
            last = jnp.where(row8 % 2 == 1, TOTAL - 1 - low, low)
            both = jnp.where(group8 < 4, m, last)
            kept = 2 * both < counts
            even = jnp.where(kept & (both % 2 == 0), 1.0, 0.0)
            odd = jnp.where(kept & (both % 2 == 1), 1.0, 0.0)
            keep_even[rows_at(TILE * tile), :] = jnp.concatenate([even, even], axis=0).astype(BF16)
            keep_odd[rows_at(TILE * tile), :] = jnp.concatenate([odd, odd], axis=0).astype(BF16)

    def prepare_last():
        @pl.loop(0, WAVES // 4)
        def _(q):
            make_rows(WAVES + q, wave_rows(4 * SLOTS * q + 4, SLOTS))

    @pl.loop(0, LEVS - 1)
    def _(i):
        d = lev_target(i)

        @pl.when(d < MIXERS)
        def _():
            lev_send(0, s1, r1, d, d, v)

    @pl.when(v < MIXERS)
    def _():
        keep_own(0, s1, r1, v, v)

    pick = (iota((256, 64), 1) == 4 * (iota((256, 64), 0) // 16) + iota((256, 64), 0) % 4).astype(BF16)
    spread = dot_nt(dot(pick, vert_ref[...]).astype(BF16), pick)
    same = (iota((256, 256), 0) // 4) % 4 == (iota((256, 256), 1) // 4) % 4
    mixm[...] = jnp.where(same, spread, 0.0).astype(BF16)

    prepare(0, 24)
    row = iota((160, 160), 0)
    column = iota((160, 160), 1)
    sel_out[...] = (column == group_row(row, row // 80)).astype(BF16)
    sel_in[...] = (row == group_row(column, column // 80)).astype(BF16)

    @pl.when(v < MIXERS)
    def _():
        landed(0, r1)
        s2[...] = dot(mixm[...], r1[...]).astype(BF16)

        @pl.loop(0, LEVS - 1)
        def _(i):
            d = lev_target(i)
            lev_send(1, s2, r2, d, d, v)

        keep_own(1, s2, r2, v, v)

    @pl.loop(1, 8)
    def _(i):
        across = 8 * lax.rem(major + i, 8) + minor
        pl.semaphore_signal(ready, 1, device_id={"wave": across}, device_id_type=MESH)

    prepare(24, 48)
    dr, dc = iota((1024, 256), 0), iota((1024, 256), 1)
    wanted = 16 * (dr // 64) + 8 * ((dr // 2) % 2) + 2 * ((dr // 16) % 4) + dr % 2
    dup[...] = (dc == wanted).astype(BF16)
    dup_one[...] = dup[0:256, 0:128]
    landed(1, r2)
    leg_copy.wait()

    for s in range(SLOTS):
        low = pair_ref[SLOTS * w + s]
        pieces = []
        corner = None
        for chunk in range(6):
            if chunk < 5:
                a = r2[40 * s + 8 * chunk : 40 * s + 8 * chunk + 8, :].astype(F32)
            else:
                a = r2[200:208, :].astype(F32)
            r = lane8 + 128 * chunk if chunk < 5 else jnp.full((8, 128), TOTAL, jnp.int32)
            first = r < TOTAL - low
            gap = jnp.where(first, r, r - TOTAL + low)
            sign = jnp.where(gap % 2 == 0, 1.0, -1.0)
            t0 = jnp.where(first, a, 0.0)
            t1 = jnp.where(first, 0.0, a)
            quad = jnp.concatenate([t0, t0 * sign, t1, t1 * sign], axis=0)
            if chunk < 5:
                pieces.append(quad.astype(BF16))
            else:
                corner = quad[:, s : s + 1]
        coefs = jnp.concatenate(pieces, axis=1)
        last_row = leg_v[s, TOTAL : TOTAL + 1, :].astype(F32)
        total = dot(coefs, leg_v[s, 0:TOTAL, :]) + corner * last_row
        fb[32 * s : 32 * s + 32, :] = total.astype(BF16)

    f = dot(sel_out[...], fb[...])
    lane = iota((32, 768), 1) // BAND % 5
    blank = jnp.zeros((32, 128), F32)
    shifted = []
    for g in range(5):
        part = jnp.concatenate([f[16 * g : 16 * g + 16], f[80 + 16 * g : 96 + 16 * g]], axis=0)
        wide = jnp.concatenate([part, blank], axis=1)
        shifted.append(wide if g == 0 else pltpu.roll(wide, BAND * g, axis=1))
    for beta in range(5):
        merged = shifted[0]
        for g in range(1, 5):
            merged = jnp.where(lane == (g + beta) % 5, shifted[g], merged)
        hs[32 * beta : 32 * beta + 32, :] = merged

    group = w // TILE
    chip, core = lax.rem(w, TILE) // 2, lax.rem(w, 2)

    def wave_send(phase, source, target, k, d):
        pltpu.make_async_remote_copy(
            src_ref=source.at[rows_at(TILE * d)],
            dst_ref=target.at[rows_at(TILE * w)],
            send_sem=send_sem.at[phase],
            recv_sem=recv_sem.at[2 + GROUPS * (phase - 2) + k],
            device_id={"wave": d},
            device_id_type=MESH,
        ).start()

    def window_of(b):
        start = BAND * b
        aligned = (start // 128) * 128
        return pl.ds(pl.multiple_of(aligned, 128), 256), start - aligned

    def mirror(band):
        upper = band < WAVES // 2
        return jnp.where(upper, band, WAVES - 1 - band), jnp.where(upper, 0, TILE), upper

    def cut(d):
        b, south, _ = mirror(d)
        lanes, offset = window_of(b)
        window = hs[rows_at(32 * lax.rem(b, 5) + south), lanes]
        message = pltpu.roll(window, lax.rem(256 - offset, 256), axis=1)[:, 0:128].astype(BF16)
        s3[rows_at(TILE * d), :] = message

    def target_of(k, j):
        return (
            TILE * lax.rem(group + ORDER[k], GROUPS)
            + 2 * lax.rem(chip + far_first(j // 2), 8)
            + lax.rem(core + j, 2)
        )

    def send_group(phase, source, target, k):
        @pl.loop(0, TILE if k + 1 < GROUPS else TILE - 2)
        def _(j):
            wave_send(phase, source, target, k, target_of(k, j))

        if k + 1 == GROUPS:
            wave_send(phase, source, target, k, target_of(k, TILE - 1))
            keep_own(2 + GROUPS * (phase - 2) + k, source, target, w, w)

    def source_group(k):
        return lax.rem(group - ORDER[k] + GROUPS, GROUPS)

    pl.semaphore_wait(ready, 7)
    for k in range(GROUPS):

        @pl.loop(0, TILE, unroll=8)
        def _(j):
            cut(target_of(k, j))

        send_group(2, s3, r3, k)

    prepare(48, WAVES)
    prepare_last()
    wind_copy.wait()

    @pl.loop(0, BAND // 2)
    def _(q):
        wind_f[q, 0:4, :] = wind_v[2 * q].astype(F32)
        wind_f[q, 4:8, :] = wind_v[2 * q + 1].astype(F32)

    qi = iota((160, 128), 0)
    ql = iota((160, 128), 1)
    lat_row = (qi % 80) // 4
    node = jnp.where(north, lat_row, BAND - 1 - lat_row)
    column_of = jnp.where(qi < 80, qi % 4, 4)
    gather = (ql == BAND * column_of + node).astype(BF16)
    level_match = iota((80, 256), 0) % 4 == (iota((80, 256), 1) // 4) % 4
    singles = [jnp.zeros((80, 256), F32)] * 2
    for k in range(GROUPS):
        block = pl.ds(pl.multiple_of(GROUP_ROWS * source_group(k), GROUP_ROWS), GROUP_ROWS)
        landed(2 + k, r3.at[block])
        for half, keep in enumerate((keep_even, keep_odd)):
            y = dot_nt(gather, r3[block, :] * keep[block, :])
            xt[80 * half : 80 * half + 80, 0:256] = y[0:80].astype(BF16)
            single = jnp.where(level_match, y[80:160], 0.0).astype(BF16)
            singles[half] = singles[half] + dot(single, dup[block, :])
        if k + 1 < GROUPS:

            for j in range(HALF // 256):
                low = pl.ds(256 * j, 256)
                term = dot(xt[:, 0:256], basis[block, low])
                acc[:, low] = acc[:, low] + term if k else term

    for half in range(2):
        xt[80 * half : 80 * half + 80, 256:512] = singles[half].astype(BF16)

    si = iota((256, 160), 0)
    sj = iota((256, 160), 1)
    half_row = si // 128
    lane_row = si % 128
    lat_nat = jnp.where(north, lane_row % BAND, BAND - 1 - lane_row % BAND)
    wanted_col = 80 * half_row + 4 * lat_nat + lane_row // BAND
    scatter = ((sj == wanted_col) & (lane_row < 80)).astype(BF16)

    for j in range(HALF // 256):
        low = pl.ds(256 * j, 256)
        high = pl.ds(HALF + 256 * j, 256)
        g = (
            acc[:, low]
            + dot(xt[:, 0:256], basis[block, low])
            + dot(xt[:, 256:512], basis[1024:COLS, low])
        )
        even, odd = g[0:80], g[80:160]
        near = (even + odd).astype(BF16).astype(F32) * wind_f[:, :, low].reshape(80, 256)
        far = (even - odd).astype(BF16).astype(F32) * wind_f[:, :, high].reshape(80, 256)
        ff[0:80, :] = (near + far).astype(BF16)
        ff[80:160, :] = (near - far).astype(BF16)
        fp[:, low] = dot(scatter, ff[...]).astype(BF16)

    zi, zl = iota((256, 128), 0), iota((256, 128), 1)
    own_level = (zl // BAND) == (zi // 4) % 4
    fold_r, fold_c = iota((128, 128), 0), iota((128, 128), 1)
    fold = ((fold_c == 80 + fold_r % BAND) & (fold_r < 80)).astype(BF16)

    def spectral_rows(rows):
        product = dot_nt(basis[rows, :], fp[...])
        return product[:, 0:128] * back_even[rows, :] + product[:, 128:256] * back_odd[rows, :]

    for k in range(GROUPS):
        target_group = lax.rem(group + ORDER[k], GROUPS)
        block = pl.ds(pl.multiple_of(GROUP_ROWS * target_group, GROUP_ROWS), GROUP_ROWS)
        main = spectral_rows(block).astype(BF16).astype(F32)
        single = spectral_rows(pl.ds(pl.multiple_of(1024 + 64 * target_group, 64), 64)).astype(BF16)
        spread_rows = jnp.where(own_level, dot(dup_one[:, 0:64], single), 0.0).astype(BF16)
        s5[block, :] = (main + dot(spread_rows, fold)).astype(BF16)
        send_group(3, s5, r5, k)

    hs[...] = jnp.zeros_like(hs)
    empty = jnp.zeros((TILE, 128), F32)
    for k in range(GROUPS):
        first_band = TILE * source_group(k)
        landed(6 + k, r5.at[rows_at(TILE * first_band, GROUP_ROWS)])

        @pl.loop(0, TILE, unroll=4)
        def _(j):
            b, _, upper = mirror(first_band + j)
            lanes, offset = window_of(b)
            message = r5[rows_at(TILE * (first_band + j)), :].astype(F32)
            placed = pltpu.roll(jnp.concatenate([message, empty], axis=1), offset, axis=1)
            at = 32 * lax.rem(b, 5)
            hs[rows_at(at), lanes] += placed
            hs[rows_at(at + TILE), lanes] += placed * jnp.where(upper, 1.0, -1.0)

    weights = qw_ref[...].reshape(1, TOTAL)
    for g in range(5):
        merged = hs[0:32, :]
        for beta in range(1, 5):
            merged = jnp.where(lane == (g + beta) % 5, hs[32 * beta : 32 * beta + 32, :], merged)
        if g:
            merged = pltpu.roll(merged, 768 - BAND * g, axis=1)
        merged = (merged[:, 0:TOTAL] * weights).astype(BF16)
        fb[16 * g : 16 * g + 16, :] = merged[0:16]
        fb[80 + 16 * g : 96 + 16 * g, :] = merged[16:32]

    folded_rows = dot(sel_in[...], fb[...]).astype(BF16)
    r_all = iota((8, TOTAL + 1), 1)
    for s in range(SLOTS):
        low = pair_ref[SLOTS * w + s]
        first = r_all < TOTAL - low
        gap = jnp.where(first, r_all, r_all - TOTAL + low)
        odd = gap % 2 == 1
        o = dot_nt(folded_rows[32 * s : 32 * s + 32], leg_v[s])
        result = jnp.where(
            first, jnp.where(odd, o[8:16], o[0:8]), jnp.where(odd, o[24:32], o[16:24])
        )
        out_ref[s, 0] = result[0:4]
        out_ref[s, 1] = result[4:8]

    @pl.when(v < MIXERS)
    def _():
        sent(0, s1.at[pl.ds(0, TILE * (MIXERS - 1))])
        sent(1, s2.at[pl.ds(0, TILE * (LEVS - 1))])

    @pl.when(v >= MIXERS)
    def _():
        sent(0, s1)

    sent(2, s3.at[pl.ds(0, TILE * (WAVES - 1))])
    sent(3, s5.at[pl.ds(0, TILE * (WAVES - 1))])


def shards(spectral, legendre, quad_weights, pair_order, lon_counts, vertical, wind_field):
    operands = (spectral, legendre, quad_weights, pair_order, lon_counts, vertical, wind_field)
    vmem = pl.BlockSpec(memory_space=pltpu.VMEM)
    hbm = pl.BlockSpec(memory_space=pltpu.HBM)
    message = pltpu.VMEM((TILE * WAVES, 128), BF16)
    tiles = pltpu.VMEM((TILE * LEVS, 128), BF16)
    return pl.pallas_call(
        kernel,
        out_shape=jax.ShapeDtypeStruct(spectral.shape, F32),
        in_specs=[hbm] * len(operands),
        out_specs=vmem,
        scratch_shapes=[
            pltpu.VMEM(spectral.shape, BF16),
            pltpu.VMEM(quad_weights.shape, F32),
            pltpu.SMEM(pair_order.shape, jnp.int32),
            pltpu.SMEM(lon_counts.shape, jnp.int32),
            pltpu.VMEM(vertical.shape, BF16),
            pltpu.VMEM(legendre.shape, BF16),
            pltpu.VMEM(wind_field.shape, BF16),
            pltpu.VMEM((BAND // 2, 8, LONS), F32),
            pltpu.VMEM((256, 256), BF16),
            pltpu.VMEM((2 * MIXERS, 8, 128), F32),
            pltpu.VMEM((TILE * MIXERS, 128), BF16),
            tiles,
            tiles,
            pltpu.VMEM((TILE * MIXERS, 128), BF16),
            pltpu.VMEM((COLS, HALF), BF16),
            message,
            message,
            pltpu.VMEM((COLS, 128), F32),
            pltpu.VMEM((COLS, 128), F32),
            pltpu.VMEM((160, TOTAL), BF16),
            pltpu.VMEM((160, 768), F32),
            pltpu.VMEM((160, 160), BF16),
            pltpu.VMEM((160, 160), BF16),
            message,
            message,
            pltpu.VMEM((160, 512), BF16),
            pltpu.VMEM((160, HALF), F32),
            pltpu.VMEM((160, 256), BF16),
            pltpu.VMEM((256, HALF), BF16),
            message,
            message,
            pltpu.VMEM((1024, 256), BF16),
            pltpu.VMEM((256, 128), BF16),
            pltpu.SemaphoreType.REGULAR,
            pltpu.SemaphoreType.DMA((7,)),
            pltpu.SemaphoreType.DMA((4,)),
            pltpu.SemaphoreType.DMA((10,)),
        ],
        compiler_params=pltpu.CompilerParams(
            collective_id=0, has_side_effects=True, vmem_limit_bytes=50 * 1024 * 1024
        ),
    )(*(pltpu.with_memory_space_constraint(x, pltpu.HBM) for x in operands))


def solution(mesh):
    return jax.shard_map(
        shards,
        mesh=mesh,
        in_specs=(
            P("wave", None, "lev", None),
            P("wave", None, None),
            P(),
            P(),
            P(),
            P(),
            P("wave", "lev", None),
        ),
        out_specs=P("wave", None, "lev", None),
        check_vma=False,
    )
```

```python
import math

import jax
import jax.numpy as jnp
from jax import lax
from jax.experimental import pallas as pl
from jax.experimental.pallas import tpu as pltpu
from jax.sharding import PartitionSpec as P

MESH = pl.DeviceIdType.MESH
F32 = jnp.float32
BF16 = jnp.bfloat16

WAVES = 64
LEVS = 16
SLOTS = 5
LEVELS = 4
TOTAL = 640
BAND = 20
LONS = 2560
HALF = LONS // 2
TILE = 16
MIXERS = 13
GROUPS = 4
ORDER = (2, 1, 3, 0)
GROUP_ROWS = TILE * WAVES // GROUPS
COLS = 2 * SLOTS * 2 * WAVES


def dot(a, b):
    return jnp.dot(a, b, preferred_element_type=F32)


def dot_nt(a, b):
    return lax.dot_general(a, b, (((1,), (1,)), ((), ())), preferred_element_type=F32)


def iota(shape, dim):
    return lax.broadcasted_iota(jnp.int32, shape, dim)


def rows_at(start, size=TILE):
    return pl.ds(pl.multiple_of(start, TILE), size)


def half_angle(phase):
    wrapped = phase - float(LONS) * jnp.floor(phase * (1.0 / LONS) + 0.5)
    u = wrapped * (math.pi / LONS)
    q = u * u
    sine = u * (
        1.0
        + q * (-1 / 6 + q * (1 / 120 + q * (-1 / 5040 + q * (1 / 362880 + q * (-1 / 39916800)))))
    )
    cosine = 1.0 + q * (
        -1 / 2
        + q * (1 / 24 + q * (-1 / 720 + q * (1 / 40320 + q * (-1 / 3628800 + q * (1 / 479001600)))))
    )
    return 1.0 - 2.0 * sine * sine, 2.0 * sine * cosine


def group_row(row, half):
    g, rho = (row - 80 * half) // TILE, row % TILE
    last = g == 4
    s = jnp.where(last, 4, (rho // 2) % 4)
    t = rho % 2
    c = jnp.where(last, (rho // 2) % 2, rho // 8)
    level = jnp.where(last, rho // 4, g)
    return 32 * s + 16 * t + 8 * half + 4 * c + level


def kernel(
    spec_hbm,
    leg_hbm,
    qw_hbm,
    pair_hbm,
    cnt_hbm,
    vert_hbm,
    wind_hbm,
    out_ref,
    spec_ref,
    qw_ref,
    pair_ref,
    cnt_ref,
    vert_ref,
    leg_v,
    wind_v,
    wind_f,
    mixm,
    s1f,
    s1,
    r1,
    s2,
    r2,
    basis,
    keep_even,
    keep_odd,
    back_even,
    back_odd,
    fb,
    hs,
    sel_out,
    sel_in,
    s3,
    r3,
    xt,
    acc,
    ff,
    fp,
    s5,
    r5,
    dup,
    dup_one,
    ready,
    local_sem,
    send_sem,
    recv_sem,
):
    w = lax.axis_index("wave")
    v = lax.axis_index("lev")
    north = w < WAVES // 2

    small = (
        (spec_hbm, spec_ref),
        (vert_hbm, vert_ref),
        (pair_hbm, pair_ref),
        (cnt_hbm, cnt_ref),
        (qw_hbm, qw_ref),
    )
    loads = [
        pltpu.make_async_copy(source, target, local_sem.at[2 + i])
        for i, (source, target) in enumerate(small)
    ]
    for copy in loads:
        copy.start()

    barrier = pltpu.get_barrier_semaphore()

    @pl.loop(1, LEVS, unroll=True)
    def _(i):
        pl.semaphore_signal(barrier, 1, device_id={"lev": lax.rem(v + i, LEVS)}, device_id_type=MESH)

    major, minor = w // 8, w % 8

    @pl.loop(1, 8, unroll=True)
    def _(i):
        across = 8 * lax.rem(major + i, 8) + minor
        pl.semaphore_signal(barrier, 1, device_id={"wave": across}, device_id_type=MESH)
        along = 8 * major + lax.rem(minor + i, 8)
        pl.semaphore_signal(barrier, 1, device_id={"wave": along}, device_id_type=MESH)

    for copy in loads:
        copy.wait()
    leg_copy = pltpu.make_async_copy(leg_hbm, leg_v, local_sem.at[0])
    leg_copy.start()
    wind_copy = pltpu.make_async_copy(wind_hbm, wind_v, local_sem.at[1])
    wind_copy.start()

    first_lane = iota((LEVELS, 128), 1)

    @pl.loop(0, SLOTS)
    def _(s):
        for c in range(2):
            for chunk in range(5):
                piece = spec_ref[s, c, :, 128 * chunk : 128 * chunk + 128].astype(F32)
                s1f[5 * s + chunk, 4 * c : 4 * c + 4, :] = piece

    for c in range(2):
        piece = jnp.zeros((LEVELS, 128), F32)
        for s in range(SLOTS):
            column = spec_ref[s, c, :, TOTAL : TOTAL + 1].astype(F32)
            piece = jnp.where(first_lane == s, jnp.broadcast_to(column, (LEVELS, 128)), piece)
        s1f[25, 4 * c : 4 * c + 4, :] = piece
    s1[...] = s1f[...].reshape(TILE * MIXERS, 128).astype(BF16)

    pl.semaphore_wait(barrier, LEVS - 1 + 14)

    def far_first(i):
        return 4 + ((i + 1) // 2) * (1 - 2 * lax.rem(i, 2))

    def lev_target(i):
        return 2 * lax.rem(v // 2 + far_first(i // 2), 8) + lax.rem(v + i + 1, 2)

    def lev_send(phase, source, target, d, here, there):
        pltpu.make_async_remote_copy(
            src_ref=source.at[rows_at(TILE * here)],
            dst_ref=target.at[rows_at(TILE * there)],
            send_sem=send_sem.at[phase],
            recv_sem=recv_sem.at[phase],
            device_id={"lev": d},
            device_id_type=MESH,
        ).start()

    def keep_own(phase, source, target, here, there):
        pltpu.make_async_copy(
            source.at[rows_at(TILE * here)], target.at[rows_at(TILE * there)], recv_sem.at[phase]
        ).start()

    def landed(phase, part):
        pltpu.make_async_copy(part, part, recv_sem.at[phase]).wait()

    def sent(phase, part):
        pltpu.make_async_copy(part, part, send_sem.at[phase]).wait()

    lane8 = iota((8, 128), 1)
    row8 = iota((8, 128), 0)
    group8 = lane8 // BAND
    lat_of = lane8 % BAND
    counts = jnp.zeros((8, 128), jnp.int32)
    for jj in range(BAND):
        lat = jnp.where(north, BAND * w + jj, BAND * w + BAND - 1 - jj)
        counts = jnp.where(lat_of == jj, cnt_ref[lat], counts)
    counts = jnp.where(group8 < 5, counts, 0)

    def wave_rows(first, stride):
        m = jnp.zeros((8, 128), jnp.int32)
        for i in range(4):
            m = jnp.where(row8 // 2 == i, pair_ref[first + stride * i], m)
        return jnp.where(row8 % 2 == 1, TOTAL - 1 - m, m)

    def make_rows(tile, m):
        mf = m.astype(F32)
        factor = jnp.where(m == 0, 1.0, 2.0)
        cos0, sin0 = half_angle(mf * lane8.astype(F32))
        turn_c, turn_s = half_angle(mf * 128.0)
        real, imag = factor * cos0, -factor * sin0
        for a in range(HALF // 128):
            basis[rows_at(TILE * tile), 128 * a : 128 * a + 128] = jnp.concatenate(
                [real, imag], axis=0
            ).astype(BF16)
            if a + 1 < HALF // 128:
                real, imag = real * turn_c + imag * turn_s, imag * turn_c - real * turn_s
        kept = (2 * m < counts) & (group8 < 4)
        scale = jnp.where(m == 0, 1.0 / LONS, 1.0 / (2 * LONS))
        even = jnp.where(kept & (m % 2 == 0), scale, 0.0)
        odd = jnp.where(kept & (m % 2 == 1), scale, 0.0)
        back_even[rows_at(TILE * tile), :] = jnp.concatenate([even, even], axis=0)
        back_odd[rows_at(TILE * tile), :] = jnp.concatenate([odd, odd], axis=0)

    def prepare(start, stop):
        @pl.loop(start, stop)
        def _(tile):
            m = wave_rows(SLOTS * tile, 1)
            make_rows(tile, m)
            low = pair_ref[SLOTS * tile + 4]
            last = jnp.where(row8 % 2 == 1, TOTAL - 1 - low, low)
            both = jnp.where(group8 < 4, m, last)
            kept = 2 * both < counts
            even = jnp.where(kept & (both % 2 == 0), 1.0, 0.0)
            odd = jnp.where(kept & (both % 2 == 1), 1.0, 0.0)
            keep_even[rows_at(TILE * tile), :] = jnp.concatenate([even, even], axis=0).astype(BF16)
            keep_odd[rows_at(TILE * tile), :] = jnp.concatenate([odd, odd], axis=0).astype(BF16)

    def prepare_last():
        @pl.loop(0, WAVES // 4)
        def _(q):
            make_rows(WAVES + q, wave_rows(4 * SLOTS * q + 4, SLOTS))

    @pl.loop(0, LEVS - 1, unroll=True)
    def _(i):
        d = lev_target(i)

        @pl.when(d < MIXERS)
        def _():
            lev_send(0, s1, r1, d, d, v)

    @pl.when(v < MIXERS)
    def _():
        keep_own(0, s1, r1, v, v)

    pick = (iota((256, 64), 1) == 4 * (iota((256, 64), 0) // 16) + iota((256, 64), 0) % 4).astype(BF16)
    spread = dot_nt(dot(pick, vert_ref[...]).astype(BF16), pick)
    same = (iota((256, 256), 0) // 4) % 4 == (iota((256, 256), 1) // 4) % 4
    mixm[...] = jnp.where(same, spread, 0.0).astype(BF16)

    prepare(0, 24)
    row = iota((160, 160), 0)
    column = iota((160, 160), 1)
    sel_out[...] = (column == group_row(row, row // 80)).astype(BF16)
    sel_in[...] = (row == group_row(column, column // 80)).astype(BF16)

    @pl.when(v < MIXERS)
    def _():
        landed(0, r1)
        s2[...] = dot(mixm[...], r1[...]).astype(BF16)

        @pl.loop(0, LEVS - 1, unroll=True)
        def _(i):
            d = lev_target(i)
            lev_send(1, s2, r2, d, d, v)

        keep_own(1, s2, r2, v, v)

    @pl.loop(1, 8, unroll=True)
    def _(i):
        across = 8 * lax.rem(major + i, 8) + minor
        pl.semaphore_signal(ready, 1, device_id={"wave": across}, device_id_type=MESH)

    prepare(24, 48)
    dr, dc = iota((1024, 256), 0), iota((1024, 256), 1)
    wanted = 16 * (dr // 64) + 8 * ((dr // 2) % 2) + 2 * ((dr // 16) % 4) + dr % 2
    dup[...] = (dc == wanted).astype(BF16)
    dup_one[...] = dup[0:256, 0:128]
    landed(1, r2)
    leg_copy.wait()

    for s in range(SLOTS):
        low = pair_ref[SLOTS * w + s]
        pieces = []
        corner = None
        for chunk in range(6):
            if chunk < 5:
                a = r2[40 * s + 8 * chunk : 40 * s + 8 * chunk + 8, :].astype(F32)
            else:
                a = r2[200:208, :].astype(F32)
            r = lane8 + 128 * chunk if chunk < 5 else jnp.full((8, 128), TOTAL, jnp.int32)
            first = r < TOTAL - low
            gap = jnp.where(first, r, r - TOTAL + low)
            sign = jnp.where(gap % 2 == 0, 1.0, -1.0)
            t0 = jnp.where(first, a, 0.0)
            t1 = jnp.where(first, 0.0, a)
            quad = jnp.concatenate([t0, t0 * sign, t1, t1 * sign], axis=0)
            if chunk < 5:
                pieces.append(quad.astype(BF16))
            else:
                corner = quad[:, s : s + 1]
        coefs = jnp.concatenate(pieces, axis=1)
        last_row = leg_v[s, TOTAL : TOTAL + 1, :].astype(F32)
        total = dot(coefs, leg_v[s, 0:TOTAL, :]) + corner * last_row
        fb[32 * s : 32 * s + 32, :] = total.astype(BF16)

    f = dot(sel_out[...], fb[...])
    lane = iota((32, 768), 1) // BAND % 5
    blank = jnp.zeros((32, 128), F32)
    shifted = []
    for g in range(5):
        part = jnp.concatenate([f[16 * g : 16 * g + 16], f[80 + 16 * g : 96 + 16 * g]], axis=0)
        wide = jnp.concatenate([part, blank], axis=1)
        shifted.append(wide if g == 0 else pltpu.roll(wide, BAND * g, axis=1))
    for beta in range(5):
        merged = shifted[0]
        for g in range(1, 5):
            merged = jnp.where(lane == (g + beta) % 5, shifted[g], merged)
        hs[32 * beta : 32 * beta + 32, :] = merged

    group = w // TILE
    chip, core = lax.rem(w, TILE) // 2, lax.rem(w, 2)

    def wave_send(phase, source, target, k, d):
        pltpu.make_async_remote_copy(
            src_ref=source.at[rows_at(TILE * d)],
            dst_ref=target.at[rows_at(TILE * w)],
            send_sem=send_sem.at[phase],
            recv_sem=recv_sem.at[2 + GROUPS * (phase - 2) + k],
            device_id={"wave": d},
            device_id_type=MESH,
        ).start()

    def window_of(b):
        start = BAND * b
        aligned = (start // 128) * 128
        return pl.ds(pl.multiple_of(aligned, 128), 256), start - aligned

    def mirror(band):
        upper = band < WAVES // 2
        return jnp.where(upper, band, WAVES - 1 - band), jnp.where(upper, 0, TILE), upper

    def cut(d):
        b, south, _ = mirror(d)
        lanes, offset = window_of(b)
        window = hs[rows_at(32 * lax.rem(b, 5) + south), lanes]
        message = pltpu.roll(window, lax.rem(256 - offset, 256), axis=1)[:, 0:128].astype(BF16)
        s3[rows_at(TILE * d), :] = message

    def target_of(k, j):
        return (
            TILE * lax.rem(group + ORDER[k], GROUPS)
            + 2 * lax.rem(chip + far_first(j // 2), 8)
            + lax.rem(core + j, 2)
        )

    def send_group(phase, source, target, k):
        @pl.loop(0, TILE if k + 1 < GROUPS else TILE - 2, unroll=True)
        def _(j):
            wave_send(phase, source, target, k, target_of(k, j))

        if k + 1 == GROUPS:
            wave_send(phase, source, target, k, target_of(k, TILE - 1))
            keep_own(2 + GROUPS * (phase - 2) + k, source, target, w, w)

    def source_group(k):
        return lax.rem(group - ORDER[k] + GROUPS, GROUPS)

    pl.semaphore_wait(ready, 7)
    for k in range(GROUPS):

        @pl.loop(0, TILE, unroll=True)
        def _(j):
            cut(target_of(k, j))

        send_group(2, s3, r3, k)

    prepare(48, WAVES)
    prepare_last()
    wind_copy.wait()

    @pl.loop(0, BAND // 2)
    def _(q):
        wind_f[q, 0:4, :] = wind_v[2 * q].astype(F32)
        wind_f[q, 4:8, :] = wind_v[2 * q + 1].astype(F32)

    qi = iota((160, 128), 0)
    ql = iota((160, 128), 1)
    lat_row = (qi % 80) // 4
    node = jnp.where(north, lat_row, BAND - 1 - lat_row)
    column_of = jnp.where(qi < 80, qi % 4, 4)
    gather = (ql == BAND * column_of + node).astype(BF16)
    level_match = iota((80, 256), 0) % 4 == (iota((80, 256), 1) // 4) % 4
    singles = [jnp.zeros((80, 256), F32)] * 2
    for k in range(GROUPS):
        block = pl.ds(pl.multiple_of(GROUP_ROWS * source_group(k), GROUP_ROWS), GROUP_ROWS)
        landed(2 + k, r3.at[block])
        for half, keep in enumerate((keep_even, keep_odd)):
            y = dot_nt(gather, r3[block, :] * keep[block, :])
            xt[80 * half : 80 * half + 80, 0:256] = y[0:80].astype(BF16)
            single = jnp.where(level_match, y[80:160], 0.0).astype(BF16)
            singles[half] = singles[half] + dot(single, dup[block, :])
        if k + 1 < GROUPS:

            for j in range(HALF // 256):
                low = pl.ds(256 * j, 256)
                term = dot(xt[:, 0:256], basis[block, low])
                acc[:, low] = acc[:, low] + term if k else term

    for half in range(2):
        xt[80 * half : 80 * half + 80, 256:512] = singles[half].astype(BF16)

    si = iota((256, 160), 0)
    sj = iota((256, 160), 1)
    half_row = si // 128
    lane_row = si % 128
    lat_nat = jnp.where(north, lane_row % BAND, BAND - 1 - lane_row % BAND)
    wanted_col = 80 * half_row + 4 * lat_nat + lane_row // BAND
    scatter = ((sj == wanted_col) & (lane_row < 80)).astype(BF16)

    for j in range(HALF // 256):
        low = pl.ds(256 * j, 256)
        high = pl.ds(HALF + 256 * j, 256)
        g = (
            acc[:, low]
            + dot(xt[:, 0:256], basis[block, low])
            + dot(xt[:, 256:512], basis[1024:COLS, low])
        )
        even, odd = g[0:80], g[80:160]
        near = (even + odd).astype(BF16).astype(F32) * wind_f[:, :, low].reshape(80, 256)
        far = (even - odd).astype(BF16).astype(F32) * wind_f[:, :, high].reshape(80, 256)
        ff[0:80, :] = (near + far).astype(BF16)
        ff[80:160, :] = (near - far).astype(BF16)
        fp[:, low] = dot(scatter, ff[...]).astype(BF16)

    zi, zl = iota((256, 128), 0), iota((256, 128), 1)
    own_level = (zl // BAND) == (zi // 4) % 4
    fold_r, fold_c = iota((128, 128), 0), iota((128, 128), 1)
    fold = ((fold_c == 80 + fold_r % BAND) & (fold_r < 80)).astype(BF16)

    def spectral_rows(rows):
        product = dot_nt(basis[rows, :], fp[...])
        return product[:, 0:128] * back_even[rows, :] + product[:, 128:256] * back_odd[rows, :]

    for k in range(GROUPS):
        target_group = lax.rem(group + ORDER[k], GROUPS)
        block = pl.ds(pl.multiple_of(GROUP_ROWS * target_group, GROUP_ROWS), GROUP_ROWS)
        main = spectral_rows(block).astype(BF16).astype(F32)
        single = spectral_rows(pl.ds(pl.multiple_of(1024 + 64 * target_group, 64), 64)).astype(BF16)
        spread_rows = jnp.where(own_level, dot(dup_one[:, 0:64], single), 0.0).astype(BF16)
        s5[block, :] = (main + dot(spread_rows, fold)).astype(BF16)
        send_group(3, s5, r5, k)

    hs[...] = jnp.zeros_like(hs)
    empty = jnp.zeros((TILE, 128), F32)
    for k in range(GROUPS):
        first_band = TILE * source_group(k)
        landed(6 + k, r5.at[rows_at(TILE * first_band, GROUP_ROWS)])

        @pl.loop(0, TILE, unroll=8)
        def _(j):
            b, _, upper = mirror(first_band + j)
            lanes, offset = window_of(b)
            message = r5[rows_at(TILE * (first_band + j)), :].astype(F32)
            placed = pltpu.roll(jnp.concatenate([message, empty], axis=1), offset, axis=1)
            at = 32 * lax.rem(b, 5)
            hs[rows_at(at), lanes] += placed
            hs[rows_at(at + TILE), lanes] += placed * jnp.where(upper, 1.0, -1.0)

    weights = qw_ref[...].reshape(1, TOTAL)
    for g in range(5):
        merged = hs[0:32, :]
        for beta in range(1, 5):
            merged = jnp.where(lane == (g + beta) % 5, hs[32 * beta : 32 * beta + 32, :], merged)
        if g:
            merged = pltpu.roll(merged, 768 - BAND * g, axis=1)
        merged = (merged[:, 0:TOTAL] * weights).astype(BF16)
        fb[16 * g : 16 * g + 16, :] = merged[0:16]
        fb[80 + 16 * g : 96 + 16 * g, :] = merged[16:32]

    folded_rows = dot(sel_in[...], fb[...]).astype(BF16)
    r_all = iota((8, TOTAL + 1), 1)
    for s in range(SLOTS):
        low = pair_ref[SLOTS * w + s]
        first = r_all < TOTAL - low
        gap = jnp.where(first, r_all, r_all - TOTAL + low)
        odd = gap % 2 == 1
        o = dot_nt(folded_rows[32 * s : 32 * s + 32], leg_v[s])
        result = jnp.where(
            first, jnp.where(odd, o[8:16], o[0:8]), jnp.where(odd, o[24:32], o[16:24])
        )
        out_ref[s, 0] = result[0:4]
        out_ref[s, 1] = result[4:8]

    @pl.when(v < MIXERS)
    def _():
        sent(0, s1.at[pl.ds(0, TILE * (MIXERS - 1))])
        sent(1, s2.at[pl.ds(0, TILE * (LEVS - 1))])

    @pl.when(v >= MIXERS)
    def _():
        sent(0, s1)

    sent(2, s3.at[pl.ds(0, TILE * (WAVES - 1))])
    sent(3, s5.at[pl.ds(0, TILE * (WAVES - 1))])


def shards(spectral, legendre, quad_weights, pair_order, lon_counts, vertical, wind_field):
    operands = (spectral, legendre, quad_weights, pair_order, lon_counts, vertical, wind_field)
    vmem = pl.BlockSpec(memory_space=pltpu.VMEM)
    hbm = pl.BlockSpec(memory_space=pltpu.HBM)
    message = pltpu.VMEM((TILE * WAVES, 128), BF16)
    tiles = pltpu.VMEM((TILE * LEVS, 128), BF16)
    return pl.pallas_call(
        kernel,
        out_shape=jax.ShapeDtypeStruct(spectral.shape, F32),
        in_specs=[hbm] * len(operands),
        out_specs=vmem,
        scratch_shapes=[
            pltpu.VMEM(spectral.shape, BF16),
            pltpu.VMEM(quad_weights.shape, F32),
            pltpu.SMEM(pair_order.shape, jnp.int32),
            pltpu.SMEM(lon_counts.shape, jnp.int32),
            pltpu.VMEM(vertical.shape, BF16),
            pltpu.VMEM(legendre.shape, BF16),
            pltpu.VMEM(wind_field.shape, BF16),
            pltpu.VMEM((BAND // 2, 8, LONS), F32),
            pltpu.VMEM((256, 256), BF16),
            pltpu.VMEM((2 * MIXERS, 8, 128), F32),
            pltpu.VMEM((TILE * MIXERS, 128), BF16),
            tiles,
            tiles,
            pltpu.VMEM((TILE * MIXERS, 128), BF16),
            pltpu.VMEM((COLS, HALF), BF16),
            message,
            message,
            pltpu.VMEM((COLS, 128), F32),
            pltpu.VMEM((COLS, 128), F32),
            pltpu.VMEM((160, TOTAL), BF16),
            pltpu.VMEM((160, 768), F32),
            pltpu.VMEM((160, 160), BF16),
            pltpu.VMEM((160, 160), BF16),
            message,
            message,
            pltpu.VMEM((160, 512), BF16),
            pltpu.VMEM((160, HALF), F32),
            pltpu.VMEM((160, 256), BF16),
            pltpu.VMEM((256, HALF), BF16),
            message,
            message,
            pltpu.VMEM((1024, 256), BF16),
            pltpu.VMEM((256, 128), BF16),
            pltpu.SemaphoreType.REGULAR,
            pltpu.SemaphoreType.DMA((7,)),
            pltpu.SemaphoreType.DMA((4,)),
            pltpu.SemaphoreType.DMA((10,)),
        ],
        compiler_params=pltpu.CompilerParams(
            collective_id=0, has_side_effects=True, vmem_limit_bytes=50 * 1024 * 1024
        ),
    )(*(pltpu.with_memory_space_constraint(x, pltpu.HBM) for x in operands))


def solution(mesh):
    return jax.shard_map(
        shards,
        mesh=mesh,
        in_specs=(
            P("wave", None, "lev", None),
            P("wave", None, None),
            P(),
            P(),
            P(),
            P(),
            P("wave", "lev", None),
        ),
        out_specs=P("wave", None, "lev", None),
        check_vma=False,
    )
```
